256 devices in a mesh: dom: 8 (over y_lo, x), neu: 32 (over y_hi, z, core).
Axes of the slice: x: 4, y: 4 (y_hi: 2, y_lo: 2; y = y_hi * 2 + y_lo), z: 8, core: 2. Of those that a mesh axis runs over, the one named last changes fastest.
Arguments:
- spec_label: int32 [1728], P('dom'), may hold values from 0 to 9
- spec_offset: int32 [1728], P('dom'), may hold values from 1 to 9
- class_rows: bfloat16 [10, 8192], P(None, 'neu'), may hold values from -0.0625 to 0.0625
- deep_weight: bfloat16 [8192, 8192], P(None, 'neu'), may hold values from -0.0625 to 0.0625
- deep_bias: float32 [8192], P('neu'), may hold values from -3 to 3
- deep_status: int32 [216, 8192], P('dom', 'neu'), may hold values from 0 to 2
- deep_bounds: int32 [2, 216, 8192], P(None, 'dom', 'neu'), may hold values from 1 to 16
- deep_slopes: float32 [8192], P('neu'), may hold values from 0 to 1
- first_weight: bfloat16 [8192, 3072], P(None, 'neu'), may hold values from -0.109375 to 0.109375
- first_bias: float32 [8192], P('neu'), may hold values from -3 to 3
- first_status: int32 [216, 8192], P('dom', 'neu'), may hold values from 0 to 2
- first_bounds: int32 [2, 216, 8192], P(None, 'dom', 'neu'), may hold values from 1 to 16
- first_slopes: float32 [8192], P('neu'), may hold values from 0 to 1
- box_center: float32 [3072], P('neu'), may hold values from -5 to 5
- box_radius: float32 [3072], P('neu'), may hold values from 0.02 to 0.2
Outputs:
- bound_rows: float32 [1728], P('dom')
- first_next: float32 [8192], P('neu')
- deep_next: float32 [8192], P('neu')
The draws below stay inside these ranges and needn't reach their ends.
Inputs may be any that keep to these rules, and one draw needn't show every extreme that they name: `deep_status`: 0 marks a neuron split inactive in that domain, 1 split active, 2 unsplit. `first_status`: 0 marks a neuron split inactive in that domain, 1 split active, 2 unsplit.
All inputs are finite; a program needn't handle non-finite values.
Results may differ from the reference program's by a relative error of at most 0.0017.
Values may be sent and summed in bfloat16 or wider, within the bound.
No kernel may reach another device: no remote copies, remote signals or barrier semaphores. Data moves between devices by JAX's collectives and lax.ppermute only.
A program may use at most 64 MiB of HBM per device.

```python
import math
import jax
import jax.numpy as jnp
from jax import lax

HIDDEN_SIZE = 8192
INPUTS = 3072
CLASSES = 10
DOMAINS = 216
ROWS = 1728


def set_ends(result, stream_key, smallest, largest):
    longest = result.shape.index(max(result.shape))
    spots = []
    for shift in (0, 1):
        where = [jax.random.randint(jax.random.fold_in(stream_key, axis), (), 0, length) for axis, length in enumerate(result.shape)]
        where[longest] = (where[longest] + shift) % result.shape[longest]
        spots.append(tuple(where))
    return result.at[spots[0]].set(smallest).at[spots[1]].set(largest)


def steps_of(rng, dims, split, smallest, largest):
    gain, own = 1.0, jax.random.fold_in(rng, 6)
    for position, shards_of in split:
        steps = jnp.exp(jax.random.uniform(jax.random.fold_in(own, position), (shards_of,), jnp.float32, smallest / len(split), largest / len(split)))
        gain = gain * jnp.repeat(steps, dims[position] // shards_of).reshape([-1 if axis == position else 1 for axis in range(len(dims))])
    return gain


def noise(own_key, extent, spread, most, shards=(), kind=jnp.bfloat16):
    drawn = spread * jax.random.normal(own_key, extent, jnp.float32)
    if shards:
        drawn = drawn * steps_of(own_key, extent, shards, -0.22, 0.18)
    return jnp.clip(drawn, -most, most).astype(kind)


def setup_inputs(seed: int = 0) -> dict:
    seeds = jax.random.split(jax.random.key(seed), 16)
    spec_label = set_ends(jax.random.randint(seeds[0], (ROWS,), 0, CLASSES), jax.random.fold_in(seeds[0], 1), 0, CLASSES - 1).astype(jnp.int32)
    spec_offset = set_ends(jax.random.randint(seeds[1], (ROWS,), 1, CLASSES), jax.random.fold_in(seeds[1], 1), 1, CLASSES - 1).astype(jnp.int32)
    class_rows = noise(seeds[2], (CLASSES, HIDDEN_SIZE), HIDDEN_SIZE ** -0.5, 0.0625, ((1, 32),))
    deep_weight = noise(seeds[3], (HIDDEN_SIZE, HIDDEN_SIZE), HIDDEN_SIZE ** -0.5, 0.0625, ((1, 32),))
    deep_bias = noise(seeds[4], (HIDDEN_SIZE,), 0.5, 3.0, ((0, 32),), jnp.float32)
    deep_status = set_ends(jax.random.randint(seeds[5], (DOMAINS, HIDDEN_SIZE), 0, 3), jax.random.fold_in(seeds[5], 1), 0, 2).astype(jnp.int32)
    deep_bounds = set_ends(jax.random.randint(seeds[6], (2, DOMAINS, HIDDEN_SIZE), 1, 17), jax.random.fold_in(seeds[6], 1), 1, 16).astype(jnp.int32)
    deep_slopes = jnp.clip(1.0 * jax.random.uniform(seeds[7], (HIDDEN_SIZE,), jnp.float32) ** steps_of(seeds[7], (HIDDEN_SIZE,), ((0, 32),), -0.2, 0.2), 0.0, 1.0)
    first_weight = noise(seeds[8], (HIDDEN_SIZE, INPUTS), INPUTS ** -0.5, 0.109375, ((1, 32),))
    first_bias = noise(seeds[9], (HIDDEN_SIZE,), 0.5, 3.0, ((0, 32),), jnp.float32)
    first_status = set_ends(jax.random.randint(seeds[10], (DOMAINS, HIDDEN_SIZE), 0, 3), jax.random.fold_in(seeds[10], 1), 0, 2).astype(jnp.int32)
    first_bounds = set_ends(jax.random.randint(seeds[11], (2, DOMAINS, HIDDEN_SIZE), 1, 17), jax.random.fold_in(seeds[11], 1), 1, 16).astype(jnp.int32)
    first_slopes = jnp.clip(1.0 * jax.random.uniform(seeds[12], (HIDDEN_SIZE,), jnp.float32) ** steps_of(seeds[12], (HIDDEN_SIZE,), ((0, 32),), -0.2, 0.2), 0.0, 1.0)
    box_center = noise(seeds[13], (INPUTS,), 1.0, 5.0, ((0, 32),), jnp.float32)
    box_radius = jnp.clip(jnp.exp(math.log(0.2) - 2.3025851 * jax.random.uniform(seeds[14], (INPUTS,), jnp.float32) ** steps_of(seeds[14], (INPUTS,), ((0, 32),), -0.2, 0.2)), 0.02, 0.2)
    return {"spec_label": spec_label, "spec_offset": spec_offset, "class_rows": class_rows, "deep_weight": deep_weight, "deep_bias": deep_bias, "deep_status": deep_status, "deep_bounds": deep_bounds, "deep_slopes": deep_slopes, "first_weight": first_weight, "first_bias": first_bias, "first_status": first_status, "first_bounds": first_bounds, "first_slopes": first_slopes, "box_center": box_center, "box_radius": box_radius}


grid_step = 0.0625
step_rate = 0.25
epsilon = 1e-06

def relax_layer(coeffs, status, bounds, slopes):
    domain_count = status.shape[0]
    row_count = coeffs.shape[0]
    column_count = coeffs.shape[1]
    shaped = coeffs.reshape(domain_count, row_count // domain_count, column_count)
    lower_edge = -grid_step * bounds[0].astype(jnp.float32)
    upper_edge = grid_step * bounds[1].astype(jnp.float32)
    slope_ratio = upper_edge / (upper_edge - lower_edge)
    intercept = -slope_ratio * lower_edge
    kind_codes = status[:, None, :]
    positive = shaped >= 0.0
    unstable = kind_codes == 2
    relaxed = jnp.where(positive, slopes[None, None, :], slope_ratio[:, None, :])
    factor = jnp.where(unstable, relaxed, jnp.where(kind_codes == 1, 1.0, 0.0))
    offset = jnp.where(unstable & jnp.logical_not(positive), intercept[:, None, :], 0.0)
    chosen = jnp.where(unstable & positive, 1.0, 0.0)
    shape_back = (row_count, column_count)
    return (factor.reshape(shape_back), offset.reshape(shape_back), chosen.reshape(shape_back))

def advance(slopes, gradient):
    root_mean = jnp.sqrt(jnp.mean(gradient * gradient) + epsilon)
    return jnp.clip(slopes + step_rate * gradient / root_mean, 0.0, 1.0)

def reference(spec_label, spec_offset, class_rows, deep_weight, deep_bias, deep_status, deep_bounds, deep_slopes, first_weight, first_bias, first_status, first_bounds, first_slopes, box_center, box_radius):
    classes_iota = jnp.arange(CLASSES, dtype=jnp.int32)
    second_label = (spec_label + spec_offset) % CLASSES
    select = (spec_label[:, None] == classes_iota[None, :]).astype(jnp.float32) - (second_label[:, None] == classes_iota[None, :]).astype(jnp.float32)
    deep_coeffs = jnp.dot(select.astype(jnp.bfloat16), class_rows, preferred_element_type=jnp.float32)
    deep_factor, deep_offset, deep_chosen = relax_layer(deep_coeffs, deep_status, deep_bounds, deep_slopes)
    deep_sent = (deep_coeffs * deep_factor).astype(jnp.bfloat16)
    deep_const = lax.optimization_barrier(jnp.sum(deep_sent.astype(jnp.float32) * deep_bias[None, :] + deep_coeffs * deep_offset, axis=1))
    first_coeffs = jnp.dot(deep_sent, deep_weight, preferred_element_type=jnp.float32)
    first_factor, first_offset, first_chosen = relax_layer(first_coeffs, first_status, first_bounds, first_slopes)
    first_sent = (first_coeffs * first_factor).astype(jnp.bfloat16)
    first_const = lax.optimization_barrier(jnp.sum(first_sent.astype(jnp.float32) * first_bias[None, :] + first_coeffs * first_offset, axis=1))
    input_coeffs = jnp.dot(first_sent, first_weight, preferred_element_type=jnp.float32)
    bound_rows = lax.optimization_barrier(jnp.sum(input_coeffs * box_center[None, :] - jnp.abs(input_coeffs) * box_radius[None, :], axis=1)) + first_const + deep_const
    input_grads = (box_center[None, :] - jnp.sign(input_coeffs) * box_radius[None, :]).astype(jnp.bfloat16)
    first_grads = jnp.dot(input_grads, first_weight.T, preferred_element_type=jnp.float32) + first_bias[None, :]
    first_sum = lax.optimization_barrier(jnp.sum(first_grads * first_coeffs * first_chosen, axis=0))
    back_grads = (first_grads * first_factor + first_offset).astype(jnp.bfloat16)
    deep_grads = jnp.dot(back_grads, deep_weight.T, preferred_element_type=jnp.float32) + deep_bias[None, :]
    deep_sum = lax.optimization_barrier(jnp.sum(deep_grads * deep_coeffs * deep_chosen, axis=0))
    return (bound_rows, advance(first_slopes, first_sum), advance(deep_slopes, deep_sum))
```

```python
import functools

import jax
import jax.numpy as jnp
from jax import lax
from jax.experimental import pallas as pl
from jax.experimental.pallas import tpu as pltpu
from jax.sharding import Mesh
from jax.sharding import PartitionSpec as P

HIDDEN_SIZE = 8192
CLASSES = 10
GROUP = 8
LANES = 256

grid_step = 0.0625
step_rate = 0.25
epsilon = 1e-06

ROWS_UP, ROWS_LOW, ROWS_CLASS, ROWS_ALL = 0, 32, 64, 80

DOM = ("ylo", "x")
NEU = ("yhi", "z", "core")
F32, BF16 = jnp.float32, jnp.bfloat16


def spread(per_domain):
    count, width = per_domain.shape
    return jnp.broadcast_to(per_domain[:, None, :], (count, GROUP, width)).reshape(
        count * GROUP, width
    )


def contract(left, right, left_dim, right_dim):
    return lax.dot_general(
        left, right, (((left_dim,), (right_dim,)), ((), ())), preferred_element_type=F32
    )


def selector(label, offset):
    second = label + offset
    second = jnp.where(second >= CLASSES, second - CLASSES, second)
    classes = lax.broadcasted_iota(jnp.int32, (16, label.shape[1]), 0)
    picked = jnp.where(classes == label, 1.0, 0.0) - jnp.where(classes == second, 1.0, 0.0)
    return picked.astype(BF16)


def decode(block, domains):
    up = block[ROWS_UP : ROWS_UP + 32].astype(F32)[:domains]
    low = block[ROWS_LOW : ROWS_LOW + 32].astype(F32)[:domains]
    tail = block[ROWS_CLASS:ROWS_ALL].astype(F32)
    slope = tail[10:11] + tail[11:12] + tail[12:13]
    ratio = up / (up + low)
    unsplit = (up > 0.0) & (low > 0.0)
    return up, low, ratio, slope, unsplit


def relax_rows(coeffs, status, low, up, slopes):
    ratio = up / (up + low)
    cept = ratio * (low * grid_step)
    unsplit = status == 2
    fixed = jnp.where(status == 1, 1.0, 0.0)
    at_pos = spread(jnp.where(unsplit, jnp.broadcast_to(slopes, ratio.shape), fixed))
    at_neg = spread(jnp.where(unsplit, ratio, fixed))
    off_neg = spread(jnp.where(unsplit, cept, 0.0))
    on_pos = spread(jnp.where(unsplit, 1.0, 0.0))
    positive = coeffs >= 0.0
    factor = jnp.where(positive, at_pos, at_neg)
    offset = jnp.where(positive, 0.0, off_neg)
    chosen = jnp.where(positive, on_pos, 0.0)
    return factor, offset, chosen


def forward_kernel(
    label_ref, offset_ref, a_ref, b_ref, c_ref, d_ref, weight_ref, deep_bias_ref,
    status_ref, bounds_ref, slopes_ref, bias_ref,
    sent_ref, coeffs_ref, const_ref, total, terms,
):
    step = pl.program_id(0)
    yhi, z, core = (lax.axis_index(n) for n in NEU)
    domains = status_ref.shape[0]
    select = selector(label_ref[...], offset_ref[...])

    @pl.when(step == 0)
    def _():
        total[...] = jnp.zeros_like(total)

    acc = total[...]
    for place, ref in enumerate((a_ref, b_ref, c_ref, d_ref)):
        other_y, other_core = place % 2, place // 2
        block = ref[0]
        up, low, ratio, slope, unsplit = decode(block, domains)
        coeffs = contract(select, block[ROWS_CLASS:ROWS_ALL], 0, 0)
        at_pos = jnp.where(unsplit, jnp.broadcast_to(slope, ratio.shape), ratio)
        factor = jnp.where(coeffs >= 0.0, spread(at_pos), spread(ratio))
        sent = (coeffs * factor).astype(BF16)
        if place == 0:

            @pl.when(step == z)
            def _():
                cept = jnp.where(unsplit, ratio * (low * grid_step), 0.0)
                terms[...] = sent.astype(F32) * deep_bias_ref[...] + jnp.where(
                    coeffs >= 0.0, 0.0, coeffs * spread(cept)
                )

        weight = weight_ref[yhi if not other_y else 1 - yhi, 0, core if not other_core else 1 - core]
        acc = acc + jnp.dot(sent, weight, preferred_element_type=F32)
    total[...] = acc

    @pl.when(step == pl.num_programs(0) - 1)
    def _():
        coeffs = total[...]
        factor, offset, _ = relax_rows(
            coeffs, status_ref[...], bounds_ref[0].astype(F32), bounds_ref[1].astype(F32), slopes_ref[...]
        )
        sent = (coeffs * factor).astype(BF16)
        sent_ref[...] = sent
        coeffs_ref[...] = coeffs
        summed = terms[...] + sent.astype(F32) * bias_ref[...] + coeffs * offset
        const_ref[...] = lax.dot_general(
            jnp.ones((8, summed.shape[1]), F32), summed, (((1,), (1,)), ((), ())),
            precision=lax.Precision.HIGHEST, preferred_element_type=F32,
        )


def input_kernel(a_ref, b_ref, c_ref, d_ref, w0_ref, w1_ref, w2_ref, w3_ref, out_ref, held):
    yhi, core, x = lax.axis_index("yhi"), lax.axis_index("core"), lax.axis_index("x")
    own = yhi * 2 + core
    for place, ref in enumerate((a_ref, b_ref, c_ref, d_ref)):
        held[own ^ ((place % 2) * 2 + place // 2)] = ref[...]
    zs, feats, _ = w0_ref.shape
    acc = None
    for k, ref in enumerate((w0_ref, w1_ref, w2_ref, w3_ref)):
        part = contract(ref[...].reshape(zs * feats, LANES), held[(x + 4 - k) % 4], 1, 1)
        acc = part if acc is None else acc + part
    out_ref[...] = acc.reshape(zs, feats, acc.shape[1])


def box_kernel(parts_ref, center_ref, radius_ref, const_ref, grads_ref, bound_ref):
    coeffs = parts_ref[0]
    for k in range(1, parts_ref.shape[0]):
        coeffs = coeffs + parts_ref[k]
    center, radius = center_ref[...], radius_ref[...]
    signed = jnp.where(coeffs > 0.0, radius, jnp.where(coeffs < 0.0, -radius, 0.0))
    grads = (center - signed).astype(BF16)
    for k in range(grads_ref.shape[0]):
        grads_ref[k] = grads
    terms = coeffs * center - jnp.abs(coeffs) * radius
    bound_ref[...] = jnp.sum(terms, axis=0, keepdims=True) + const_ref[0:1]


def grads_kernel(g_ref, w0_ref, w1_ref, w2_ref, w3_ref, near_ref, far_ref):
    yhi, core, x = lax.axis_index("yhi"), lax.axis_index("core"), lax.axis_index("x")
    own = yhi * 2 + core
    zs, feats, rows = g_ref.shape
    grads = g_ref[...].reshape(zs * feats, rows)
    for k, ref in enumerate((w0_ref, w1_ref, w2_ref, w3_ref)):
        part = contract(grads, ref[...].reshape(zs * feats, LANES), 0, 0)
        place = own ^ ((x + 4 - k) % 4)

        @pl.when(place % 2 == 0)
        def _():
            near_ref[place // 2] = part

        @pl.when(place % 2 == 1)
        def _():
            far_ref[place // 2] = part


def backward_kernel(
    label_ref, offset_ref, a_ref, b_ref, c_ref, d_ref, weight_ref, deep_bias_ref,
    status_ref, bounds_ref, slopes_ref, bias_ref, coeffs_ref, mine_ref, their_ref, bound_ref,
    out_ref, back,
):
    step = pl.program_id(0)
    yhi, z, core = (lax.axis_index(n) for n in NEU)
    domains = status_ref.shape[0]
    select = selector(label_ref[...], offset_ref[...])

    @pl.when(step == 0)
    def _():
        coeffs = coeffs_ref[...]
        grads = mine_ref[...] + their_ref[...].astype(F32) + bias_ref[...]
        factor, offset, chosen = relax_rows(
            coeffs, status_ref[...], bounds_ref[0].astype(F32), bounds_ref[1].astype(F32), slopes_ref[...]
        )
        back[...] = (grads * factor + offset).astype(BF16)
        out_ref[32:40] = jnp.zeros((8, LANES), F32)
        out_ref[32:33] = jnp.sum(grads * coeffs * chosen, axis=0, keepdims=True)
        out_ref[33:34, 0 : bound_ref.shape[1]] = bound_ref[...]

    for place, ref in enumerate((a_ref, b_ref, c_ref, d_ref)):
        other_y, other_core = place % 2, place // 2
        block = ref[0]
        _, _, _, _, unsplit = decode(block, domains)
        coeffs = contract(select, block[ROWS_CLASS:ROWS_ALL], 0, 0)
        mask = spread(jnp.where(unsplit, 1.0, 0.0))
        kept = jnp.maximum(coeffs, 0.0) * mask
        y = yhi if not other_y else 1 - yhi
        c = core if not other_core else 1 - core
        grads = contract(back[...], weight_ref[y, 0, c], 1, 1)
        if place == 0:
            grads = grads + jnp.where(step == z, 1.0, 0.0) * deep_bias_ref[...]
        out_ref[pl.ds((y * 8 + step) * 2 + c, 1)] = jnp.sum(grads * kept, axis=0, keepdims=True)


def whole(shape):
    return pl.BlockSpec(shape, lambda s: (0,) * len(shape))


def shifted(value, axis, size, by):
    return lax.ppermute(value, axis, [(i, (i + by) % size) for i in range(size)])


def on_device(
    spec_label, spec_offset, class_rows, deep_weight, deep_bias, deep_status, deep_bounds,
    deep_slopes, first_weight, first_bias, first_status, first_bounds, first_slopes,
    box_center, box_radius,
):
    rows = spec_label.shape[0]
    domains = deep_status.shape[0]
    feats = box_center.shape[0]
    params = pltpu.CompilerParams(vmem_limit_bytes=24 * 1024 * 1024)

    active, unsplit = deep_status == 1, deep_status == 2
    up = jnp.where(unsplit, deep_bounds[1], jnp.where(active, 1, 0))
    low = jnp.where(unsplit, deep_bounds[0], jnp.where(active, 0, 1))
    high = lax.reduce_precision(deep_slopes, 8, 7)
    rest = deep_slopes - high
    middle = lax.reduce_precision(rest, 8, 7)
    last = rest - middle
    pad = jnp.ones((32 - domains, LANES), F32)
    info = jnp.concatenate(
        [
            up.astype(F32), pad, low.astype(F32), pad, class_rows.astype(F32),
            high[None], middle[None], last[None], jnp.zeros((3, LANES), F32),
        ],
        axis=0,
    ).astype(BF16)
    x = lax.axis_index("x")
    quarter = lax.dynamic_index_in_dim(
        first_weight.reshape(2, 8, 2, LANES, feats).transpose(0, 2, 1, 3, 4).reshape(4, 8, LANES, feats),
        x, 0, keepdims=False,
    )
    message = jnp.concatenate(
        [jnp.broadcast_to(info[None], (8,) + info.shape), quarter.transpose(0, 2, 1)], axis=1
    )
    message = lax.all_to_all(message, "z", 0, 0, tiled=True)
    info_a = message[:, :ROWS_ALL]
    w_own = message[:, ROWS_ALL:]
    info_b = shifted(info_a, "yhi", 2, 1)
    info_c = shifted(info_a, "core", 2, 1)
    info_d = shifted(info_b, "core", 2, 1)
    w_all = [w_own] + [shifted(w_own, "x", 4, k) for k in (1, 2, 3)]
    infos = (info_a, info_b, info_c, info_d)

    label, offset = spec_label[None], spec_offset[None]
    weight = deep_weight.reshape(2, 8, 2, LANES, LANES)
    info_spec = pl.BlockSpec((1, ROWS_ALL, LANES), lambda s: (s, 0, 0))
    weight_spec = pl.BlockSpec((2, 1, 2, LANES, LANES), lambda s: (0, s, 0, 0, 0))
    layer_specs = [whole((domains, LANES)), whole((2, domains, LANES)), whole((1, LANES)), whole((1, LANES))]
    layer = (first_status, first_bounds, first_slopes[None], first_bias[None])

    sent, coeffs, const = pl.pallas_call(
        forward_kernel,
        grid=(8,),
        in_specs=[whole((1, rows))] * 2 + [info_spec] * 4 + [weight_spec, whole((1, LANES))] + layer_specs,
        out_specs=[whole((rows, LANES)), whole((rows, LANES)), whole((8, rows))],
        out_shape=[
            jax.ShapeDtypeStruct((rows, LANES), BF16),
            jax.ShapeDtypeStruct((rows, LANES), F32),
            jax.ShapeDtypeStruct((8, rows), F32),
        ],
        scratch_shapes=[pltpu.VMEM((rows, LANES), F32), pltpu.VMEM((rows, LANES), F32)],
        compiler_params=params,
        name="forward",
    )(label, offset, *infos, weight, deep_bias[None], *layer)

    sent_b = shifted(sent, "yhi", 2, 1)
    sent_c = shifted(sent, "core", 2, 1)
    sent_d = shifted(sent_b, "core", 2, 1)
    parts = pl.pallas_call(
        input_kernel,
        out_shape=jax.ShapeDtypeStruct((8, feats, rows), F32),
        scratch_shapes=[pltpu.VMEM((4, rows, LANES), BF16)],
        compiler_params=params,
        name="inputs",
    )(sent, sent_b, sent_c, sent_d, *w_all)
    parts = lax.all_to_all(parts, "z", 0, 0, tiled=True)
    grads, bound = pl.pallas_call(
        box_kernel,
        out_shape=[jax.ShapeDtypeStruct((8, feats, rows), BF16), jax.ShapeDtypeStruct((1, rows), F32)],
        compiler_params=params,
        name="box",
    )(parts, box_center[:, None], box_radius[:, None], const)
    grads = lax.all_to_all(grads, "z", 0, 0, tiled=True)
    near, far = pl.pallas_call(
        grads_kernel,
        out_shape=[jax.ShapeDtypeStruct((2, rows, LANES), F32)] * 2,
        compiler_params=params,
        name="grads",
    )(grads, *w_all)
    near = near + shifted(far, "core", 2, 1)
    their = shifted(near[1].astype(BF16), "yhi", 2, 1)

    summary = pl.pallas_call(
        backward_kernel,
        grid=(8,),
        in_specs=[whole((1, rows))] * 2
        + [info_spec] * 4
        + [weight_spec, whole((1, LANES))]
        + layer_specs
        + [whole((rows, LANES))] * 3
        + [whole((1, rows))],
        out_specs=whole((40, LANES)),
        out_shape=jax.ShapeDtypeStruct((40, LANES), F32),
        scratch_shapes=[pltpu.VMEM((rows, LANES), BF16)],
        compiler_params=params,
        name="backward",
    )(label, offset, *infos, weight, deep_bias[None], *layer, coeffs, near[0], their, bound)

    gathered = lax.all_to_all(jnp.broadcast_to(summary[None], (8, 40, LANES)), "z", 0, 0, tiled=True)
    sums = jnp.concatenate([jnp.sum(gathered[:, :32], axis=0), gathered[:, 32]], axis=0)
    bound = jnp.sum(gathered[:, 33], axis=0)
    moved = [shifted(sums, "x", 4, k) for k in (1, 2, 3)]
    sums = (sums + moved[1]) + (moved[0] + moved[2])
    sums = sums + shifted(sums, "ylo", 2, 1)
    first_all = sums[32:]
    first_power = jnp.sum(first_all * first_all)
    deep = jnp.concatenate([sums[:32], bound[None], jnp.full((1, LANES), first_power)], axis=0)
    deep = deep + shifted(deep, "core", 2, 1)
    deep = deep + shifted(deep, "yhi", 2, 1)
    z = lax.axis_index("z")
    own = (lax.axis_index("yhi") * 8 + z) * 2 + lax.axis_index("core")
    first_sum = lax.dynamic_index_in_dim(first_all, z, 0, keepdims=False)
    deep_sum = lax.dynamic_index_in_dim(deep, own, 0, keepdims=False)
    deep_power = jnp.sum(deep[:32] * deep[:32])

    def advance(slopes, gradient, squares):
        root_mean = jnp.sqrt(squares / HIDDEN_SIZE + epsilon)
        return jnp.clip(slopes + step_rate * gradient / root_mean, 0.0, 1.0)

    return (
        deep[32, :rows],
        advance(first_slopes, first_sum, deep[33, 0]),
        advance(deep_slopes, deep_sum, deep_power),
    )


def solution(mesh):
    fine = Mesh(mesh.devices.reshape(2, 4, 2, 8, 2), DOM + NEU)
    in_specs = (
        P(DOM), P(DOM), P(None, NEU), P(None, NEU), P(NEU), P(DOM, NEU), P(None, DOM, NEU), P(NEU),
        P(None, NEU), P(NEU), P(DOM, NEU), P(None, DOM, NEU), P(NEU), P(NEU), P(NEU),
    )
    out_specs = (P(DOM), P(NEU), P(NEU))
    return jax.shard_map(on_device, mesh=fine, in_specs=in_specs, out_specs=out_specs, check_vma=False)
```

```python
import functools

import jax
import jax.numpy as jnp
from jax import lax
from jax.experimental import pallas as pl
from jax.experimental.pallas import tpu as pltpu
from jax.sharding import Mesh
from jax.sharding import PartitionSpec as P

HIDDEN_SIZE = 8192
CLASSES = 10
GROUP = 8
LANES = 256

grid_step = 0.0625
step_rate = 0.25
epsilon = 1e-06

ROWS_UP, ROWS_LOW, ROWS_CLASS, ROWS_ALL = 0, 32, 64, 80

DOM = ("ylo", "x")
NEU = ("yhi", "z", "core")
F32, BF16 = jnp.float32, jnp.bfloat16


def spread(per_domain):
    count, width = per_domain.shape
    return jnp.broadcast_to(per_domain[:, None, :], (count, GROUP, width)).reshape(
        count * GROUP, width
    )


def contract(left, right, left_dim, right_dim):
    return lax.dot_general(
        left, right, (((left_dim,), (right_dim,)), ((), ())), preferred_element_type=F32
    )


def selector(label, offset):
    second = label + offset
    second = jnp.where(second >= CLASSES, second - CLASSES, second)
    classes = lax.broadcasted_iota(jnp.int32, (16, label.shape[1]), 0)
    picked = jnp.where(classes == label, 1.0, 0.0) - jnp.where(classes == second, 1.0, 0.0)
    return picked.astype(BF16)


def decode(block, domains):
    up = block[ROWS_UP : ROWS_UP + 32].astype(F32)[:domains]
    low = block[ROWS_LOW : ROWS_LOW + 32].astype(F32)[:domains]
    tail = block[ROWS_CLASS:ROWS_ALL].astype(F32)
    slope = tail[10:11] + tail[11:12] + tail[12:13]
    ratio = up / (up + low)
    unsplit = (up > 0.0) & (low > 0.0)
    return up, low, ratio, slope, unsplit


def relax_rows(coeffs, status, low, up, slopes):
    ratio = up / (up + low)
    cept = ratio * (low * grid_step)
    unsplit = status == 2
    fixed = jnp.where(status == 1, 1.0, 0.0)
    at_pos = spread(jnp.where(unsplit, jnp.broadcast_to(slopes, ratio.shape), fixed))
    at_neg = spread(jnp.where(unsplit, ratio, fixed))
    off_neg = spread(jnp.where(unsplit, cept, 0.0))
    on_pos = spread(jnp.where(unsplit, 1.0, 0.0))
    positive = coeffs >= 0.0
    factor = jnp.where(positive, at_pos, at_neg)
    offset = jnp.where(positive, 0.0, off_neg)
    chosen = jnp.where(positive, on_pos, 0.0)
    return factor, offset, chosen


def prep_kernel(status_ref, bounds_ref, class_ref, slopes_ref, weight_ref, out_ref, held, sems):
    x = lax.axis_index("x")
    domains = status_ref.shape[0]
    count = held.shape[0]
    copies = [
        pltpu.make_async_copy(weight_ref.at[x // 2, k, x % 2], held.at[k], sems.at[k]) for k in range(count)
    ]
    for copy in copies:
        copy.start()
    status = status_ref[...]
    active, unsplit = status == 1, status == 2
    pad = jnp.ones((32 - domains, LANES), F32)
    up = jnp.where(unsplit, bounds_ref[1], jnp.where(active, 1, 0)).astype(F32)
    low = jnp.where(unsplit, bounds_ref[0], jnp.where(active, 0, 1)).astype(F32)
    slopes = slopes_ref[...]
    high = lax.reduce_precision(slopes, 8, 7)
    middle = lax.reduce_precision(slopes - high, 8, 7)
    last = (slopes - high) - middle
    tail = jnp.concatenate([class_ref[...].astype(F32), high, middle, last, jnp.zeros((3, LANES), F32)], axis=0)
    info = jnp.concatenate([up, pad, low, pad, tail], axis=0).astype(BF16)
    for k in range(count):
        out_ref[k, 0:ROWS_ALL] = info
    for k, copy in enumerate(copies):
        copy.wait()
        out_ref[k, ROWS_ALL : ROWS_ALL + held.shape[2]] = held[k].astype(F32).T.astype(BF16)


def forward_half(
    last, label_ref, offset_ref, own_ref, other_ref, weight_ref, total, keep_terms,
):
    step = pl.program_id(0)
    core, z = lax.axis_index("core"), lax.axis_index("z")
    domains = label_ref.shape[1] // GROUP
    select = selector(label_ref[...], offset_ref[...])
    acc = total[...]
    for k in range(own_ref.shape[0]):
        for ref, side in ((own_ref, core), (other_ref, 1 - core)):
            block = ref[k]
            up, low, ratio, slope, unsplit = decode(block, domains)
            coeffs = contract(select, block[ROWS_CLASS:ROWS_ALL], 0, 0)
            at_pos = jnp.where(unsplit, jnp.broadcast_to(slope, ratio.shape), ratio)
            factor = jnp.where(coeffs >= 0.0, spread(at_pos), spread(ratio))
            sent = (coeffs * factor).astype(BF16)
            if keep_terms is not None and ref is own_ref:

                @pl.when(step * own_ref.shape[0] + k == z)
                def _():
                    keep_terms(coeffs, sent, ratio, low, unsplit)

            acc = acc + jnp.dot(sent, weight_ref[0, k, side], preferred_element_type=F32)
    total[...] = acc


def near_kernel(label_ref, offset_ref, own_ref, other_ref, weight_ref, deep_bias_ref, total_ref, terms_ref):
    @pl.when(pl.program_id(0) == 0)
    def _():
        total_ref[...] = jnp.zeros_like(total_ref)

    def keep_terms(coeffs, sent, ratio, low, unsplit):
        cept = jnp.where(unsplit, ratio * (low * grid_step), 0.0)
        terms_ref[...] = sent.astype(F32) * deep_bias_ref[...] + jnp.where(
            coeffs >= 0.0, 0.0, coeffs * spread(cept)
        )

    forward_half(False, label_ref, offset_ref, own_ref, other_ref, weight_ref, total_ref, keep_terms)


def far_kernel(
    label_ref, offset_ref, own_ref, other_ref, weight_ref, so_far_ref, terms_ref,
    status_ref, bounds_ref, slopes_ref, bias_ref, sent_ref, coeffs_ref, const_ref, total,
):
    @pl.when(pl.program_id(0) == 0)
    def _():
        total[...] = so_far_ref[...]

    forward_half(True, label_ref, offset_ref, own_ref, other_ref, weight_ref, total, None)

    @pl.when(pl.program_id(0) == pl.num_programs(0) - 1)
    def _():
        coeffs = total[...]
        factor, offset, _ = relax_rows(
            coeffs, status_ref[...], bounds_ref[0].astype(F32), bounds_ref[1].astype(F32), slopes_ref[...]
        )
        sent = (coeffs * factor).astype(BF16)
        sent_ref[...] = sent
        coeffs_ref[...] = coeffs
        const_ref[...] = row_sums(terms_ref[...] + sent.astype(F32) * bias_ref[...] + coeffs * offset)


def row_sums(values):
    return lax.dot_general(
        jnp.ones((8, values.shape[1]), F32), values, (((1,), (1,)), ((), ())),
        precision=lax.Precision.HIGHEST, preferred_element_type=F32,
    )


def hold(held, refs, own):
    for place, ref in enumerate(refs):
        held[own ^ ((place % 2) * 2 + place // 2)] = ref[...]


def input_kernel(a_ref, b_ref, c_ref, d_ref, weight_ref, out_ref, held):
    own = lax.axis_index("yhi") * 2 + lax.axis_index("core")
    hold(held, (a_ref, b_ref, c_ref, d_ref), own)
    _, zs, feats, _ = weight_ref.shape
    acc = None
    for q in range(4):
        part = contract(weight_ref[q].reshape(zs * feats, LANES), held[q], 1, 1)
        acc = part if acc is None else acc + part
    out_ref[...] = acc.reshape(zs, feats, acc.shape[1]).astype(BF16)


def column(row):
    count = row.shape[1]
    down = lax.broadcasted_iota(jnp.int32, (count, count), 0)
    across = lax.broadcasted_iota(jnp.int32, (count, count), 1)
    return jnp.sum(jnp.where(down == across, row, 0.0), axis=1, keepdims=True)


def box_kernel(parts_ref, center_ref, radius_ref, const_ref, grads_ref, bound_ref):
    coeffs = parts_ref[0].astype(F32)
    for k in range(1, parts_ref.shape[0]):
        coeffs = coeffs + parts_ref[k].astype(F32)
    center, radius = column(center_ref[...]), column(radius_ref[...])
    wide = center - jnp.where(coeffs > 0.0, radius, jnp.where(coeffs < 0.0, -radius, 0.0))
    grads = wide.astype(BF16)
    for k in range(grads_ref.shape[0]):
        grads_ref[k] = grads
    rest = coeffs * (wide - grads.astype(F32))
    bound_ref[...] = jnp.sum(rest, axis=0, keepdims=True) + const_ref[0:1]


def grads_kernel(
    g_ref, weight_ref, a_ref, b_ref, c_ref, d_ref, so_far_ref, near_ref, far_ref, bound_ref, held
):
    own = lax.axis_index("yhi") * 2 + lax.axis_index("core")
    hold(held, (a_ref, b_ref, c_ref, d_ref), own)
    zs, feats, rows = g_ref.shape
    grads = g_ref[...].reshape(zs * feats, rows)
    terms = None
    for q in range(4):
        part = contract(grads, weight_ref[q].reshape(zs * feats, LANES), 0, 0)
        term = part * held[q].astype(F32)
        terms = term if terms is None else terms + term
        place = own ^ q

        @pl.when(place % 2 == 0)
        def _():
            near_ref[place // 2] = part

        @pl.when(place % 2 == 1)
        def _():
            far_ref[place // 2] = part

    bound_ref[...] = row_sums(terms) + so_far_ref[...]


def backward_kernel(
    label_ref, offset_ref, a_ref, b_ref, c_ref, d_ref, weight_ref, deep_bias_ref,
    status_ref, bounds_ref, slopes_ref, bias_ref, coeffs_ref, near_ref, got_ref, their_ref, bound_ref,
    mine_ref, other_ref, back,
):
    step = pl.program_id(0)
    yhi, z, core = (lax.axis_index(n) for n in NEU)
    domains = status_ref.shape[0]
    select = selector(label_ref[...], offset_ref[...])

    @pl.when(step == 0)
    def _():
        coeffs = coeffs_ref[...]
        grads = near_ref[0] + got_ref[0] + their_ref[...].astype(F32) + bias_ref[...]
        factor, offset, chosen = relax_rows(
            coeffs, status_ref[...], bounds_ref[0].astype(F32), bounds_ref[1].astype(F32), slopes_ref[...]
        )
        back[...] = (grads * factor + offset).astype(BF16)
        mine_ref[16:24] = jnp.zeros((8, LANES), F32)
        mine_ref[16:17] = jnp.sum(grads * coeffs * chosen, axis=0, keepdims=True)
        mine_ref[17:18, 0 : bound_ref.shape[1]] = bound_ref[0:1]

    zs = a_ref.shape[0]
    for k in range(zs):
        for place, ref in enumerate((a_ref, b_ref, c_ref, d_ref)):
            y = yhi if place % 2 == 0 else 1 - yhi
            c = core if place // 2 == 0 else 1 - core
            block = ref[k]
            _, _, _, _, unsplit = decode(block, domains)
            coeffs = contract(select, block[ROWS_CLASS:ROWS_ALL], 0, 0)
            kept = jnp.maximum(coeffs, 0.0) * spread(jnp.where(unsplit, 1.0, 0.0))
            grads = contract(back[...], weight_ref[y, k, c], 1, 1)
            if place == 0:
                grads = grads + jnp.where(step * zs + k == z, 1.0, 0.0) * deep_bias_ref[...]
            out = mine_ref if place // 2 == 0 else other_ref
            out[pl.ds(y * 8 + step * zs + k, 1)] = jnp.sum(grads * kept, axis=0, keepdims=True)


def send_z_kernel(mine_ref, got_ref, out_ref):
    deep = mine_ref[0:16] + got_ref[...]
    rest = mine_ref[16:24]
    for k in range(out_ref.shape[0]):
        out_ref[k, 0:16] = deep
        out_ref[k, 16:24] = rest


def send_dom_kernel(got_ref, out_ref, bound_ref):
    total = got_ref[0]
    for k in range(1, got_ref.shape[0]):
        total = total + got_ref[k]
    bound_ref[...] = total[17:18]
    first = jnp.concatenate([got_ref[k, 16:17] for k in range(got_ref.shape[0])], axis=0)
    for k in range(out_ref.shape[0]):
        out_ref[k, 0:16] = total[0:16]
        out_ref[k, 16:24] = first


def send_y_kernel(got_ref, bound_ref, out_ref, first_ref):
    total = got_ref[0]
    for k in range(1, got_ref.shape[0]):
        total = total + got_ref[k]
    first = total[16:24]
    first_ref[...] = first
    out_ref[0:16] = total[0:16]
    out_ref[16:24] = jnp.zeros((8, LANES), F32)
    out_ref[16:17] = bound_ref[...]
    out_ref[17:18] = jnp.broadcast_to(jnp.sum(first * first, keepdims=True), (1, LANES))


def send_core_kernel(mine_ref, got_ref, out_ref, deep_ref):
    deep = mine_ref[0:16] + got_ref[0:16]
    deep_ref[...] = deep
    out_ref[...] = mine_ref[16:24] + got_ref[16:24]
    out_ref[2:3] = jnp.broadcast_to(jnp.sum(deep * deep, keepdims=True), (1, LANES))


def finish_kernel(mine_ref, got_ref, deep_ref, first_ref, deep_slopes_ref, first_slopes_ref, bound_ref, first_out, deep_out):
    yhi, z = lax.axis_index("yhi"), lax.axis_index("z")
    total = mine_ref[...] + got_ref[...]
    bound_ref[...] = total[0:1, 0 : bound_ref.shape[1]]

    def advance(slopes, gradient, squares):
        root_mean = jnp.sqrt(squares / HIDDEN_SIZE + epsilon)
        return jnp.clip(slopes + step_rate * gradient / root_mean, 0.0, 1.0)

    first_out[...] = advance(first_slopes_ref[...], first_ref[pl.ds(z, 1)], total[1:2])
    deep_out[...] = advance(deep_slopes_ref[...], deep_ref[pl.ds(yhi * 8 + z, 1)], total[2:3])


def whole(shape):
    return pl.BlockSpec(shape, lambda s: (0,) * len(shape))


def shape(dims, kind=F32):
    return jax.ShapeDtypeStruct(dims, kind)


def shifted(value, axis, size, by):
    return lax.ppermute(value, axis, [(i, (i + by) % size) for i in range(size)])


def on_device(
    spec_label, spec_offset, class_rows, deep_weight, deep_bias, deep_status, deep_bounds,
    deep_slopes, first_weight, first_bias, first_status, first_bounds, first_slopes,
    box_center, box_radius,
):
    rows = spec_label.shape[0]
    domains = deep_status.shape[0]
    feats = box_center.shape[0]
    params = pltpu.CompilerParams(vmem_limit_bytes=24 * 1024 * 1024)
    call = functools.partial(pl.pallas_call, compiler_params=params)
    vmem = pl.BlockSpec(memory_space=pltpu.VMEM)

    message = call(
        prep_kernel,
        in_specs=[vmem] * 4 + [pl.BlockSpec(memory_space=pl.ANY)],
        out_specs=vmem,
        out_shape=shape((8, ROWS_ALL + feats, LANES), BF16),
        scratch_shapes=[pltpu.VMEM((8, LANES, feats), BF16), pltpu.SemaphoreType.DMA((8,))],
        name="prep",
    )(deep_status, deep_bounds, class_rows, deep_slopes[None], first_weight.reshape(2, 8, 2, LANES, feats))
    message = lax.all_to_all(message, "z", 0, 0, tiled=True)
    info_a = message[:, :ROWS_ALL]
    info_b = shifted(info_a, "yhi", 2, 1)
    info_c = shifted(info_a, "core", 2, 1)
    info_d = shifted(info_b, "core", 2, 1)
    w_all = lax.all_gather(message[:, ROWS_ALL:], "x", axis=0)

    label, offset = spec_label[None], spec_offset[None]
    weight = deep_weight.reshape(2, 8, 2, LANES, LANES)
    depth = 2
    info_spec = pl.BlockSpec((depth, ROWS_ALL, LANES), lambda s: (s, 0, 0))
    label_specs = [whole((1, rows))] * 2
    layer_specs = [whole((domains, LANES)), whole((2, domains, LANES)), whole((1, LANES)), whole((1, LANES))]
    layer = (first_status, first_bounds, first_slopes[None], first_bias[None])
    half_spec = lambda other: pl.BlockSpec(
        (1, depth, 2, LANES, LANES), lambda s: (lax.axis_index("yhi") ^ other, s, 0, 0, 0)
    )
    square = whole((rows, LANES))

    total, terms = call(
        near_kernel,
        grid=(8 // depth,),
        in_specs=label_specs + [info_spec] * 2 + [half_spec(0), whole((1, LANES))],
        out_specs=[square, square],
        out_shape=[shape((rows, LANES)), shape((rows, LANES))],
        name="forward_near",
    )(label, offset, info_a, info_c, weight, deep_bias[None])
    sent, coeffs, const = call(
        far_kernel,
        grid=(8 // depth,),
        in_specs=label_specs + [info_spec] * 2 + [half_spec(1), square, square] + layer_specs,
        out_specs=[square, square, whole((8, rows))],
        out_shape=[shape((rows, LANES), BF16), shape((rows, LANES)), shape((8, rows))],
        scratch_shapes=[pltpu.VMEM((rows, LANES), F32)],
        name="forward_far",
    )(label, offset, info_b, info_d, weight, total, terms, *layer)

    sent_b = shifted(sent, "yhi", 2, 1)
    sent_c = shifted(sent, "core", 2, 1)
    sent_d = shifted(sent_b, "core", 2, 1)
    sents = (sent, sent_b, sent_c, sent_d)
    held = [pltpu.VMEM((4, rows, LANES), BF16)]
    parts = call(
        input_kernel, out_shape=shape((8, feats, rows), BF16), scratch_shapes=held, name="inputs"
    )(*sents, w_all)
    parts = lax.all_to_all(parts, "z", 0, 0, tiled=True)
    grads, bound = call(
        box_kernel, out_shape=[shape((8, feats, rows), BF16), shape((1, rows))], name="box"
    )(parts, box_center[None], box_radius[None], const)
    grads = lax.all_to_all(grads, "z", 0, 0, tiled=True)
    near, far, bound = call(
        grads_kernel,
        out_shape=[shape((2, rows, LANES))] * 2 + [shape((8, rows))],
        scratch_shapes=held,
        name="grads",
    )(grads, w_all, *sents, bound)
    got = shifted(far, "core", 2, 1)
    their = shifted((near[1] + got[1]).astype(BF16), "yhi", 2, 1)

    first_of_two = pl.BlockSpec((1, rows, LANES), lambda s: (0, 0, 0))
    mine, other = call(
        backward_kernel,
        grid=(8 // depth,),
        in_specs=label_specs
        + [info_spec] * 4
        + [pl.BlockSpec((2, depth, 2, LANES, LANES), lambda s: (0, s, 0, 0, 0)), whole((1, LANES))]
        + layer_specs
        + [square, first_of_two, first_of_two, square, whole((8, rows))],
        out_specs=[whole((24, LANES)), whole((16, LANES))],
        out_shape=[shape((24, LANES)), shape((16, LANES))],
        scratch_shapes=[pltpu.VMEM((rows, LANES), BF16)],
        name="backward",
    )(label, offset, info_a, info_b, info_c, info_d, weight, deep_bias[None], *layer, coeffs, near, got, their, bound)

    to_all = shape((8, 24, LANES))
    to_z = call(send_z_kernel, out_shape=to_all, name="send_z")(mine, shifted(other, "core", 2, 1))
    got = lax.all_to_all(to_z, "z", 0, 0, tiled=True)
    to_dom, bound = call(send_dom_kernel, out_shape=[to_all, shape((1, LANES))], name="send_dom")(got)
    got = lax.all_to_all(to_dom, DOM, 0, 0, tiled=True)
    to_y, first = call(
        send_y_kernel, out_shape=[shape((24, LANES)), shape((8, LANES))], name="send_y"
    )(got, bound)
    to_core, deep = call(
        send_core_kernel, out_shape=[shape((8, LANES)), shape((16, LANES))], name="send_core"
    )(to_y, shifted(to_y, "yhi", 2, 1))
    bound, first_next, deep_next = call(
        finish_kernel, out_shape=[shape((1, rows)), shape((1, LANES)), shape((1, LANES))], name="finish"
    )(to_core, shifted(to_core, "core", 2, 1), deep, first, deep_slopes[None], first_slopes[None])
    return bound[0], first_next[0], deep_next[0]


def solution(mesh):
    fine = Mesh(mesh.devices.reshape(2, 4, 2, 8, 2), DOM + NEU)
    in_specs = (
        P(DOM), P(DOM), P(None, NEU), P(None, NEU), P(NEU), P(DOM, NEU), P(None, DOM, NEU), P(NEU),
        P(None, NEU), P(NEU), P(DOM, NEU), P(None, DOM, NEU), P(NEU), P(NEU), P(NEU),
    )
    out_specs = (P(DOM), P(NEU), P(NEU))
    return jax.shard_map(on_device, mesh=fine, in_specs=in_specs, out_specs=out_specs, check_vma=False)
```

```python
import functools

import jax
import jax.numpy as jnp
from jax import lax
from jax.experimental import pallas as pl
from jax.experimental.pallas import tpu as pltpu
from jax.sharding import Mesh
from jax.sharding import PartitionSpec as P

HIDDEN_SIZE = 8192
CLASSES = 10
GROUP = 8
LANES = 256
LIMIT = 16 * 1024 * 1024

grid_step = 0.0625
step_rate = 0.25
epsilon = 1e-06

ROWS_UP, ROWS_LOW, ROWS_CLASS, ROWS_ALL = 0, 32, 64, 80

DOM = ("ylo", "x")
NEU = ("yhi", "z", "core")
F32, BF16 = jnp.float32, jnp.bfloat16


def spread(per_domain):
    count, width = per_domain.shape
    return jnp.broadcast_to(per_domain[:, None, :], (count, GROUP, width)).reshape(
        count * GROUP, width
    )


def contract(left, right, left_dim, right_dim):
    return lax.dot_general(
        left, right, (((left_dim,), (right_dim,)), ((), ())), preferred_element_type=F32
    )


def selector(label, offset):
    second = label + offset
    second = jnp.where(second >= CLASSES, second - CLASSES, second)
    classes = lax.broadcasted_iota(jnp.int32, (16, label.shape[1]), 0)
    picked = jnp.where(classes == label, 1.0, 0.0) - jnp.where(classes == second, 1.0, 0.0)
    return picked.astype(BF16)


def decode(block, domains):
    up = block[ROWS_UP : ROWS_UP + 32].astype(F32)[:domains]
    low = block[ROWS_LOW : ROWS_LOW + 32].astype(F32)[:domains]
    tail = block[ROWS_CLASS:ROWS_ALL].astype(F32)
    slope = tail[10:11] + tail[11:12] + tail[12:13]
    ratio = up / (up + low)
    unsplit = (up > 0.0) & (low > 0.0)
    return up, low, ratio, slope, unsplit


def relax_rows(coeffs, status, low, up, slopes):
    ratio = up / (up + low)
    cept = ratio * (low * grid_step)
    unsplit = status == 2
    fixed = jnp.where(status == 1, 1.0, 0.0)
    at_pos = spread(jnp.where(unsplit, jnp.broadcast_to(slopes, ratio.shape), fixed))
    at_neg = spread(jnp.where(unsplit, ratio, fixed))
    off_neg = spread(jnp.where(unsplit, cept, 0.0))
    on_pos = spread(jnp.where(unsplit, 1.0, 0.0))
    positive = coeffs >= 0.0
    factor = jnp.where(positive, at_pos, at_neg)
    offset = jnp.where(positive, 0.0, off_neg)
    chosen = jnp.where(positive, on_pos, 0.0)
    return factor, offset, chosen


def prep_kernel(status_ref, bounds_ref, class_ref, slopes_ref, weight_ref, out_ref, status, bounds, sems):
    x = lax.axis_index("x")
    domains = status_ref.shape[0]
    count, feats = out_ref.shape[0], weight_ref.shape[0]
    firsts = [
        pltpu.make_async_copy(status_ref, status, sems.at[count]),
        pltpu.make_async_copy(bounds_ref, bounds, sems.at[count + 1]),
    ]
    copies = [
        pltpu.make_async_copy(
            weight_ref.at[:, pl.ds(pl.multiple_of(((x // 2 * count + k) * 2 + x % 2) * LANES, LANES), LANES)],
            out_ref.at[k, pl.ds(ROWS_ALL, feats)],
            sems.at[k],
        )
        for k in range(count)
    ]
    for copy in firsts + copies:
        copy.start()
    slopes = slopes_ref[...]
    high = lax.reduce_precision(slopes, 8, 7)
    middle = lax.reduce_precision(slopes - high, 8, 7)
    last = (slopes - high) - middle
    tail = jnp.concatenate([class_ref[...].astype(F32), high, middle, last, jnp.zeros((3, LANES), F32)], axis=0)
    for copy in firsts:
        copy.wait()
    active, unsplit = status[...] == 1, status[...] == 2
    pad = jnp.ones((32 - domains, LANES), F32)
    up = jnp.where(unsplit, bounds[:, 1], jnp.where(active, 1, 0)).astype(F32)
    low = jnp.where(unsplit, bounds[:, 0], jnp.where(active, 0, 1)).astype(F32)
    info = jnp.concatenate([up, pad, low, pad, tail], axis=0).astype(BF16)
    for k in range(count):
        out_ref[k, 0:ROWS_ALL] = info
    for copy in copies:
        copy.wait()


def forward_half(
    last, label_ref, offset_ref, own_ref, other_ref, weight_ref, total, keep_terms,
):
    step = pl.program_id(0)
    core, z = lax.axis_index("core"), lax.axis_index("z")
    domains = label_ref.shape[1] // GROUP
    select = selector(label_ref[...], offset_ref[...])
    acc = total[...]
    for k in range(own_ref.shape[0]):
        for ref, side in ((own_ref, core), (other_ref, 1 - core)):
            block = ref[k]
            up, low, ratio, slope, unsplit = decode(block, domains)
            coeffs = contract(select, block[ROWS_CLASS:ROWS_ALL], 0, 0)
            at_pos = jnp.where(unsplit, jnp.broadcast_to(slope, ratio.shape), ratio)
            factor = jnp.where(coeffs >= 0.0, spread(at_pos), spread(ratio))
            sent = (coeffs * factor).astype(BF16)
            if keep_terms is not None and ref is own_ref:

                @pl.when(step * own_ref.shape[0] + k == z)
                def _():
                    keep_terms(coeffs, sent, ratio, low, unsplit)

            acc = acc + jnp.dot(sent, weight_ref[0, k, side], preferred_element_type=F32)
    total[...] = acc


def near_kernel(label_ref, offset_ref, own_ref, other_ref, weight_ref, deep_bias_ref, total_ref, terms_ref):
    @pl.when(pl.program_id(0) == 0)
    def _():
        total_ref[...] = jnp.zeros_like(total_ref)

    def keep_terms(coeffs, sent, ratio, low, unsplit):
        cept = jnp.where(unsplit, ratio * (low * grid_step), 0.0)
        terms_ref[...] = sent.astype(F32) * deep_bias_ref[...] + jnp.where(
            coeffs >= 0.0, 0.0, coeffs * spread(cept)
        )

    forward_half(False, label_ref, offset_ref, own_ref, other_ref, weight_ref, total_ref, keep_terms)


def far_kernel(
    label_ref, offset_ref, own_ref, other_ref, weight_ref, so_far_ref, terms_ref,
    status_ref, bounds_ref, slopes_ref, bias_ref, sent_ref, coeffs_ref, const_ref, total,
):
    @pl.when(pl.program_id(0) == 0)
    def _():
        total[...] = so_far_ref[...]

    forward_half(True, label_ref, offset_ref, own_ref, other_ref, weight_ref, total, None)

    @pl.when(pl.program_id(0) == pl.num_programs(0) - 1)
    def _():
        coeffs = total[...]
        factor, offset, _ = relax_rows(
            coeffs, status_ref[...], bounds_ref[:, 0].astype(F32), bounds_ref[:, 1].astype(F32), slopes_ref[...]
        )
        sent = (coeffs * factor).astype(BF16)
        sent_ref[...] = sent
        coeffs_ref[...] = coeffs
        const_ref[...] = row_sums(terms_ref[...] + sent.astype(F32) * bias_ref[...] + coeffs * offset)


def row_sums(values):
    return lax.dot_general(
        jnp.ones((8, values.shape[1]), F32), values, (((1,), (1,)), ((), ())),
        precision=lax.Precision.HIGHEST, preferred_element_type=F32,
    )


def hold(held, refs, own):
    for place, ref in enumerate(refs):
        held[own ^ ((place % 2) * 2 + place // 2)] = ref[...]


SHIFTS = (0, 1, 3, 2)


def input_kernel(a_ref, b_ref, c_ref, d_ref, w0_ref, w1_ref, w2_ref, w3_ref, out_ref, held):
    own, x = lax.axis_index("yhi") * 2 + lax.axis_index("core"), lax.axis_index("x")
    hold(held, (a_ref, b_ref, c_ref, d_ref), own)
    zs, feats, _ = w0_ref.shape
    acc = None
    for by, ref in zip(SHIFTS, (w0_ref, w1_ref, w2_ref, w3_ref)):
        part = contract(ref[...].reshape(zs * feats, LANES), held[(x + 4 - by) % 4], 1, 1)
        acc = part if acc is None else acc + part
    out_ref[...] = acc.reshape(zs, feats, acc.shape[1]).astype(BF16)


def column(row):
    count = row.shape[1]
    down = lax.broadcasted_iota(jnp.int32, (count, count), 0)
    across = lax.broadcasted_iota(jnp.int32, (count, count), 1)
    return jnp.sum(jnp.where(down == across, row, 0.0), axis=1, keepdims=True)


def box_kernel(parts_ref, center_ref, radius_ref, const_ref, grads_ref, bound_ref):
    coeffs = parts_ref[0].astype(F32)
    for k in range(1, parts_ref.shape[0]):
        coeffs = coeffs + parts_ref[k].astype(F32)
    center, radius = column(center_ref[...]), column(radius_ref[...])
    wide = center - jnp.where(coeffs > 0.0, radius, jnp.where(coeffs < 0.0, -radius, 0.0))
    grads = wide.astype(BF16)
    for k in range(grads_ref.shape[0]):
        grads_ref[k] = grads
    rest = coeffs * (wide - grads.astype(F32))
    bound_ref[...] = jnp.sum(rest, axis=0, keepdims=True) + const_ref[0:1]


def grads_kernel(
    g_ref, w0_ref, w1_ref, w2_ref, w3_ref, a_ref, b_ref, c_ref, d_ref, so_far_ref,
    near_ref, far_ref, bound_ref, held,
):
    own, x = lax.axis_index("yhi") * 2 + lax.axis_index("core"), lax.axis_index("x")
    hold(held, (a_ref, b_ref, c_ref, d_ref), own)
    zs, feats, rows = g_ref.shape
    grads = g_ref[...].reshape(zs * feats, rows)
    terms = None
    for by, ref in zip(SHIFTS, (w0_ref, w1_ref, w2_ref, w3_ref)):
        q = (x + 4 - by) % 4
        part = contract(grads, ref[...].reshape(zs * feats, LANES), 0, 0)
        term = part * held[q].astype(F32)
        terms = term if terms is None else terms + term
        place = own ^ q

        @pl.when(place % 2 == 0)
        def _():
            near_ref[place // 2] = part

        @pl.when(place % 2 == 1)
        def _():
            far_ref[place // 2] = part

    bound_ref[...] = row_sums(terms) + so_far_ref[...]


def backward_kernel(
    label_ref, offset_ref, a_ref, b_ref, c_ref, d_ref, weight_ref, deep_bias_ref,
    status_ref, bounds_ref, slopes_ref, bias_ref, coeffs_ref, near_ref, got_ref, their_ref, bound_ref,
    mine_ref, other_ref, back,
):
    step = pl.program_id(0)
    yhi, z, core = (lax.axis_index(n) for n in NEU)
    domains = status_ref.shape[0]
    select = selector(label_ref[...], offset_ref[...])

    @pl.when(step == 0)
    def _():
        coeffs = coeffs_ref[...]
        grads = near_ref[0] + got_ref[0] + their_ref[...].astype(F32) + bias_ref[...]
        factor, offset, chosen = relax_rows(
            coeffs, status_ref[...], bounds_ref[:, 0].astype(F32), bounds_ref[:, 1].astype(F32), slopes_ref[...]
        )
        back[...] = (grads * factor + offset).astype(BF16)
        mine_ref[16:24] = jnp.zeros((8, LANES), F32)
        mine_ref[16:17] = jnp.sum(grads * coeffs * chosen, axis=0, keepdims=True)
        mine_ref[17:18, 0 : bound_ref.shape[1]] = bound_ref[0:1]

    zs = a_ref.shape[0]
    for k in range(zs):
        for place, ref in enumerate((a_ref, b_ref, c_ref, d_ref)):
            y = yhi if place % 2 == 0 else 1 - yhi
            c = core if place // 2 == 0 else 1 - core
            block = ref[k]
            _, _, _, _, unsplit = decode(block, domains)
            coeffs = contract(select, block[ROWS_CLASS:ROWS_ALL], 0, 0)
            kept = jnp.maximum(coeffs, 0.0) * spread(jnp.where(unsplit, 1.0, 0.0))
            grads = contract(back[...], weight_ref[y, k, c], 1, 1)
            if place == 0:
                grads = grads + jnp.where(step * zs + k == z, 1.0, 0.0) * deep_bias_ref[...]
            out = mine_ref if place // 2 == 0 else other_ref
            out[pl.ds(y * 8 + step * zs + k, 1)] = jnp.sum(grads * kept, axis=0, keepdims=True)


def send_z_kernel(mine_ref, got_ref, out_ref):
    deep = mine_ref[0:16] + got_ref[...]
    rest = mine_ref[16:24]
    for k in range(out_ref.shape[0]):
        out_ref[k, 0:16] = deep
        out_ref[k, 16:24] = rest


def send_dom_kernel(got_ref, out_ref):
    total = got_ref[0]
    for k in range(1, got_ref.shape[0]):
        total = total + got_ref[k]
    first = jnp.concatenate([got_ref[k, 16:17] for k in range(got_ref.shape[0])], axis=0)
    for k in range(out_ref.shape[0]):
        out_ref[k, 0:16] = total[0:16]
        out_ref[k, 16:24] = first
        out_ref[k, 24:32] = total[16:24]


def send_core_kernel(got_ref, out_ref, deep_ref, first_ref):
    yhi, dom = lax.axis_index("yhi"), lax.axis_index("ylo") * 4 + lax.axis_index("x")
    halves = []
    for y in range(2):
        total = got_ref[y, 0:24]
        for k in range(1, got_ref.shape[0] // 2):
            total = total + got_ref[2 * k + y, 0:24]
        halves.append(total)
    deep = halves[0][0:16] + halves[1][0:16]
    deep_ref[...] = deep
    firsts = [half[16:24] for half in halves]
    first_ref[...] = jnp.where(yhi == 0, firsts[0], firsts[1])
    power = jnp.sum(firsts[0] * firsts[0] + firsts[1] * firsts[1], keepdims=True)
    out_ref[...] = jnp.zeros_like(out_ref)
    out_ref[0:1] = (got_ref[2 * dom] + got_ref[2 * dom + 1])[25:26]
    out_ref[1:2] = jnp.broadcast_to(power, (1, LANES))
    out_ref[2:3] = jnp.broadcast_to(jnp.sum(deep * deep, keepdims=True), (1, LANES))


def finish_kernel(mine_ref, got_ref, deep_ref, first_ref, deep_slopes_ref, first_slopes_ref, bound_ref, first_out, deep_out):
    yhi, z = lax.axis_index("yhi"), lax.axis_index("z")
    total = mine_ref[...] + got_ref[...]
    bound_ref[...] = total[0:1, 0 : bound_ref.shape[1]]

    def advance(slopes, gradient, squares):
        root_mean = jnp.sqrt(squares / HIDDEN_SIZE + epsilon)
        return jnp.clip(slopes + step_rate * gradient / root_mean, 0.0, 1.0)

    first_out[...] = advance(first_slopes_ref[...], first_ref[pl.ds(z, 1)], total[1:2])
    deep_out[...] = advance(deep_slopes_ref[...], deep_ref[pl.ds(yhi * 8 + z, 1)], total[2:3])


def whole(shape):
    return pl.BlockSpec(shape, lambda s: (0,) * len(shape))


def shape(dims, kind=F32):
    return jax.ShapeDtypeStruct(dims, kind)


def shifted(value, axis, size, by):
    return lax.ppermute(value, axis, [(i, (i + by) % size) for i in range(size)])


def on_device(
    spec_label, spec_offset, class_rows, deep_weight, deep_bias, deep_status, deep_bounds,
    deep_slopes, first_weight, first_bias, first_status, first_bounds, first_slopes,
    box_center, box_radius,
):
    rows = spec_label.shape[0]
    domains = deep_status.shape[0]
    feats = box_center.shape[0]
    call = functools.partial(
        pl.pallas_call, compiler_params=pltpu.CompilerParams(vmem_limit_bytes=LIMIT)
    )
    vmem, hbm = pl.BlockSpec(), pl.BlockSpec(memory_space=pltpu.HBM)

    message = pl.pallas_call(
        prep_kernel,
        compiler_params=pltpu.CompilerParams(vmem_limit_bytes=62 * 1024 * 1024),
        in_specs=[hbm, hbm, vmem, vmem, hbm],
        out_specs=vmem,
        out_shape=shape((8, ROWS_ALL + feats, LANES), BF16),
        scratch_shapes=[
            pltpu.VMEM((domains, LANES), jnp.int32),
            pltpu.VMEM((domains, 2, LANES), jnp.int32),
            pltpu.SemaphoreType.DMA((10,)),
        ],
        name="prep",
    )(deep_status, deep_bounds.transpose(1, 0, 2), class_rows, deep_slopes[None], first_weight.T)
    message = lax.all_to_all(message, "z", 0, 0, tiled=True)
    info_a = message[:, :ROWS_ALL]
    info_b = shifted(info_a, "yhi", 2, 1)
    info_c = shifted(info_a, "core", 2, 1)
    w_own = message[:, ROWS_ALL:]
    w_all = [w_own] + [shifted(w_own, "x", 4, k) for k in SHIFTS[1:]]

    label, offset = spec_label[None], spec_offset[None]
    weight = deep_weight.reshape(2, 8, 2, LANES, LANES)
    depth = 2
    info_spec = pl.BlockSpec((depth, ROWS_ALL, LANES), lambda s: (s, 0, 0))
    label_specs = [whole((1, rows))] * 2
    layer_specs = [whole((domains, LANES)), whole((domains, 2, LANES)), whole((1, LANES)), whole((1, LANES))]
    layer = (first_status, first_bounds.transpose(1, 0, 2), first_slopes[None], first_bias[None])
    half_spec = lambda other: pl.BlockSpec(
        (1, depth, 2, LANES, LANES), lambda s: (lax.axis_index("yhi") ^ other, s, 0, 0, 0)
    )
    square = whole((rows, LANES))

    total, terms = call(
        near_kernel,
        grid=(8 // depth,),
        in_specs=label_specs + [info_spec] * 2 + [half_spec(0), whole((1, LANES))],
        out_specs=[square, square],
        out_shape=[shape((rows, LANES)), shape((rows, LANES))],
        name="forward_near",
    )(label, offset, info_a, info_c, weight, deep_bias[None])
    total, info_b, w_all[1], w_all[2] = lax.optimization_barrier((total, info_b, w_all[1], w_all[2]))
    info_d = shifted(info_b, "core", 2, 1)
    sent, coeffs, const = call(
        far_kernel,
        grid=(8 // depth,),
        in_specs=label_specs + [info_spec] * 2 + [half_spec(1), square, square] + layer_specs,
        out_specs=[square, square, whole((8, rows))],
        out_shape=[shape((rows, LANES), BF16), shape((rows, LANES)), shape((8, rows))],
        scratch_shapes=[pltpu.VMEM((rows, LANES), F32)],
        name="forward_far",
    )(label, offset, info_b, info_d, weight, total, terms, *layer)

    sent_b = shifted(sent, "yhi", 2, 1)
    sent_c = shifted(sent, "core", 2, 1)
    sent_d = shifted(sent_b, "core", 2, 1)
    sents = (sent, sent_b, sent_c, sent_d)
    held = [pltpu.VMEM((4, rows, LANES), BF16)]
    parts = call(
        input_kernel, out_shape=shape((8, feats, rows), BF16), scratch_shapes=held, name="inputs"
    )(*sents, *w_all)
    parts = lax.all_to_all(parts, "z", 0, 0, tiled=True)
    grads, bound = call(
        box_kernel, out_shape=[shape((8, feats, rows), BF16), shape((1, rows))], name="box"
    )(parts, box_center[None], box_radius[None], const)
    grads = lax.all_to_all(grads, "z", 0, 0, tiled=True)
    near, far, bound = call(
        grads_kernel,
        out_shape=[shape((2, rows, LANES))] * 2 + [shape((8, rows))],
        scratch_shapes=held,
        name="grads",
    )(grads, *w_all, *sents, bound)
    got = shifted(far, "core", 2, 1)
    their = shifted((near[1] + got[1]).astype(BF16), "yhi", 2, 1)

    first_of_two = pl.BlockSpec((1, rows, LANES), lambda s: (0, 0, 0))
    mine, other = call(
        backward_kernel,
        grid=(8 // depth,),
        in_specs=label_specs
        + [info_spec] * 4
        + [pl.BlockSpec((2, depth, 2, LANES, LANES), lambda s: (0, s, 0, 0, 0)), whole((1, LANES))]
        + layer_specs
        + [square, first_of_two, first_of_two, square, whole((8, rows))],
        out_specs=[whole((24, LANES)), whole((16, LANES))],
        out_shape=[shape((24, LANES)), shape((16, LANES))],
        scratch_shapes=[pltpu.VMEM((rows, LANES), BF16)],
        name="backward",
    )(label, offset, info_a, info_b, info_c, info_d, weight, deep_bias[None], *layer, coeffs, near, got, their, bound)

    to_z = call(send_z_kernel, out_shape=shape((8, 24, LANES)), name="send_z")(mine, shifted(other, "core", 2, 1))
    got = lax.all_to_all(to_z, "z", 0, 0, tiled=True)
    to_dom = call(send_dom_kernel, out_shape=shape((16, 32, LANES)), name="send_dom")(got)
    got = lax.all_to_all(to_dom, DOM + ("yhi",), 0, 0, tiled=True)
    to_core, deep, first = call(
        send_core_kernel,
        out_shape=[shape((8, LANES)), shape((16, LANES)), shape((8, LANES))],
        name="send_core",
    )(got)
    bound, first_next, deep_next = call(
        finish_kernel, out_shape=[shape((1, rows)), shape((1, LANES)), shape((1, LANES))], name="finish"
    )(to_core, shifted(to_core, "core", 2, 1), deep, first, deep_slopes[None], first_slopes[None])
    return bound[0], first_next[0], deep_next[0]


def solution(mesh):
    fine = Mesh(mesh.devices.reshape(2, 4, 2, 8, 2), DOM + NEU)
    in_specs = (
        P(DOM), P(DOM), P(None, NEU), P(None, NEU), P(NEU), P(DOM, NEU), P(None, DOM, NEU), P(NEU),
        P(None, NEU), P(NEU), P(DOM, NEU), P(None, DOM, NEU), P(NEU), P(NEU), P(NEU),
    )
    out_specs = (P(DOM), P(NEU), P(NEU))
    return jax.shard_map(on_device, mesh=fine, in_specs=in_specs, out_specs=out_specs, check_vma=False)
```

```python
import functools

import jax
import jax.numpy as jnp
from jax import lax
from jax.experimental import pallas as pl
from jax.experimental.pallas import tpu as pltpu
from jax.sharding import Mesh
from jax.sharding import PartitionSpec as P

HIDDEN_SIZE = 8192
CLASSES = 10
GROUP = 8
LANES = 256
LIMIT = 16 * 1024 * 1024

grid_step = 0.0625
step_rate = 0.25
epsilon = 1e-06

ROWS_ALL = 72
CLASS_ROWS = ((0, 30, 2), (2, 59, 5), (7, 64, 3))

DOM = ("ylo", "x")
NEU = ("yhi", "z", "core")
F32, BF16 = jnp.float32, jnp.bfloat16


def spread(per_domain):
    count, width = per_domain.shape
    return jnp.broadcast_to(per_domain[:, None, :], (count, GROUP, width)).reshape(
        count * GROUP, width
    )


def contract(left, right, left_dim, right_dim):
    return lax.dot_general(
        left, right, (((left_dim,), (right_dim,)), ((), ())), preferred_element_type=F32
    )


def selector(label, offset):
    second = label + offset
    second = jnp.where(second >= CLASSES, second - CLASSES, second)
    rows = lax.broadcasted_iota(jnp.int32, (ROWS_ALL, label.shape[1]), 0)
    classes = jnp.full_like(rows, -1)
    for first, at, count in CLASS_ROWS:
        classes = jnp.where((rows >= at) & (rows < at + count), rows - at + first, classes)
    picked = jnp.where(classes == label, 1.0, 0.0) - jnp.where(classes == second, 1.0, 0.0)
    return picked.astype(BF16)


def pieces(values):
    high = lax.reduce_precision(values, 8, 7)
    middle = lax.reduce_precision(values - high, 8, 7)
    return high, middle, (values - high) - middle


def clamped(status, low, up):
    active, unsplit = status == 1, status == 2
    up = jnp.where(unsplit, up, jnp.where(active, 1, 0)).astype(F32)
    low = jnp.where(unsplit, low, jnp.where(active, 0, 1)).astype(F32)
    return low, up


def compose(low, up, classes, slopes):
    return jnp.concatenate(
        [up, *pieces(slopes), classes[0:2], low, classes[2:10], jnp.zeros((5, LANES), F32)], axis=0
    ).astype(BF16)


def decode(block, domains):
    wide = block.astype(F32)
    up, low = wide[0:32][:domains], wide[32:64][:domains]
    slope = wide[27:28] + wide[28:29] + wide[29:30]
    ratio = up / (up + low)
    unsplit = (up > 0.0) & (low > 0.0)
    return up, low, ratio, slope, unsplit


def relax_rows(coeffs, status, low, up, slopes):
    ratio = up / (up + low)
    cept = ratio * (low * grid_step)
    unsplit = status == 2
    fixed = jnp.where(status == 1, 1.0, 0.0)
    at_pos = spread(jnp.where(unsplit, jnp.broadcast_to(slopes, ratio.shape), fixed))
    at_neg = spread(jnp.where(unsplit, ratio, fixed))
    off_neg = spread(jnp.where(unsplit, cept, 0.0))
    on_pos = spread(jnp.where(unsplit, 1.0, 0.0))
    positive = coeffs >= 0.0
    factor = jnp.where(positive, at_pos, at_neg)
    offset = jnp.where(positive, 0.0, off_neg)
    chosen = jnp.where(positive, on_pos, 0.0)
    return factor, offset, chosen


def prep_kernel(status_ref, bounds_ref, class_ref, slopes_ref, weight_ref, out_ref, status, bounds, sems):
    x = lax.axis_index("x")
    count, feats = out_ref.shape[0], weight_ref.shape[0]
    firsts = [
        pltpu.make_async_copy(status_ref, status, sems.at[count]),
        pltpu.make_async_copy(bounds_ref, bounds, sems.at[count + 1]),
    ]
    copies = [
        pltpu.make_async_copy(
            weight_ref.at[:, pl.ds(pl.multiple_of(((x // 2 * count + k) * 2 + x % 2) * LANES, LANES), LANES)],
            out_ref.at[k, pl.ds(0, feats)],
            sems.at[k],
        )
        for k in range(count)
    ]
    for copy in firsts + copies:
        copy.start()
    for copy in firsts:
        copy.wait()
    low, up = clamped(status[...], bounds[:, 0], bounds[:, 1])
    info = compose(low, up, class_ref[...].astype(F32), slopes_ref[...])
    for k in range(count):
        out_ref[k, feats : feats + ROWS_ALL] = info
    for copy in copies:
        copy.wait()


def forward_half(label_ref, offset_ref, own_ref, other_ref, weight_ref, total):
    core = lax.axis_index("core")
    domains = label_ref.shape[1] // GROUP
    select = selector(label_ref[...], offset_ref[...])
    acc = total[...]
    for k in range(own_ref.shape[0]):
        for ref, side in ((own_ref, core), (other_ref, 1 - core)):
            block = ref[k]
            _, _, ratio, slope, unsplit = decode(block, domains)
            coeffs = contract(select, block, 0, 0)
            at_pos = jnp.where(unsplit, jnp.broadcast_to(slope, ratio.shape), ratio)
            factor = jnp.where(coeffs >= 0.0, spread(at_pos), spread(ratio))
            sent = (coeffs * factor).astype(BF16)
            acc = acc + jnp.dot(sent, weight_ref[0, k, side], preferred_element_type=F32)
    total[...] = acc


def own_kernel(label_ref, offset_ref, info_ref, bias_ref, const_ref, extra_ref):
    domains = label_ref.shape[1] // GROUP
    block = info_ref[lax.axis_index("z")]
    _, low, ratio, slope, unsplit = decode(block, domains)
    coeffs = contract(selector(label_ref[...], offset_ref[...]), block, 0, 0)
    at_pos = jnp.where(unsplit, jnp.broadcast_to(slope, ratio.shape), ratio)
    positive = coeffs >= 0.0
    sent = (coeffs * jnp.where(positive, spread(at_pos), spread(ratio))).astype(BF16)
    cept = spread(jnp.where(unsplit, ratio * (low * grid_step), 0.0))
    const_ref[...] = row_sums(sent.astype(F32) * bias_ref[...] + jnp.where(positive, 0.0, coeffs * cept))
    kept = jnp.maximum(coeffs, 0.0) * spread(jnp.where(unsplit, 1.0, 0.0))
    extra_ref[...] = jnp.sum(kept, axis=0, keepdims=True) * bias_ref[...]


def near_kernel(label_ref, offset_ref, own_ref, other_ref, weight_ref, total_ref):
    @pl.when(pl.program_id(0) == 0)
    def _():
        total_ref[...] = jnp.zeros_like(total_ref)

    forward_half(label_ref, offset_ref, own_ref, other_ref, weight_ref, total_ref)


def far_kernel(
    label_ref, offset_ref, own_ref, other_ref, weight_ref, so_far_ref, own_const_ref,
    status_ref, bounds_ref, slopes_ref, bias_ref, sent_ref, coeffs_ref, const_ref, total,
):
    @pl.when(pl.program_id(0) == 0)
    def _():
        total[...] = so_far_ref[...]

    forward_half(label_ref, offset_ref, own_ref, other_ref, weight_ref, total)

    @pl.when(pl.program_id(0) == pl.num_programs(0) - 1)
    def _():
        coeffs = total[...]
        factor, offset, _ = relax_rows(
            coeffs, status_ref[...], bounds_ref[:, 0].astype(F32), bounds_ref[:, 1].astype(F32), slopes_ref[...]
        )
        sent = (coeffs * factor).astype(BF16)
        sent_ref[...] = sent
        coeffs_ref[...] = coeffs
        const_ref[...] = own_const_ref[...] + row_sums(sent.astype(F32) * bias_ref[...] + coeffs * offset)


def row_sums(values):
    return lax.dot_general(
        jnp.ones((8, values.shape[1]), F32), values, (((1,), (1,)), ((), ())),
        precision=lax.Precision.HIGHEST, preferred_element_type=F32,
    )


def hold(held, refs, own):
    for place, ref in enumerate(refs):
        held[own ^ ((place % 2) * 2 + place // 2)] = ref[...]


SHIFTS = (0, 1, 3, 2)


def input_kernel(a_ref, b_ref, c_ref, d_ref, w0_ref, w1_ref, w2_ref, w3_ref, out_ref, held):
    own, x = lax.axis_index("yhi") * 2 + lax.axis_index("core"), lax.axis_index("x")
    hold(held, (a_ref, b_ref, c_ref, d_ref), own)
    zs, feats, _ = w0_ref.shape
    acc = None
    for by, ref in zip(SHIFTS, (w0_ref, w1_ref, w2_ref, w3_ref)):
        part = contract(ref[...].reshape(zs * feats, LANES), held[(x + 4 - by) % 4], 1, 1)
        acc = part if acc is None else acc + part
    out_ref[...] = acc.reshape(zs, feats, acc.shape[1]).astype(BF16)


def column(row):
    count = row.shape[1]
    down = lax.broadcasted_iota(jnp.int32, (count, count), 0)
    across = lax.broadcasted_iota(jnp.int32, (count, count), 1)
    return jnp.sum(jnp.where(down == across, row, 0.0), axis=1, keepdims=True)


def box_kernel(parts_ref, center_ref, radius_ref, const_ref, grads_ref, bound_ref):
    coeffs = parts_ref[0].astype(F32)
    for k in range(1, parts_ref.shape[0]):
        coeffs = coeffs + parts_ref[k].astype(F32)
    center, radius = column(center_ref[...]), column(radius_ref[...])
    wide = center - jnp.where(coeffs > 0.0, radius, jnp.where(coeffs < 0.0, -radius, 0.0))
    grads = wide.astype(BF16)
    for k in range(grads_ref.shape[0]):
        grads_ref[k] = grads
    rest = coeffs * (wide - grads.astype(F32))
    bound_ref[...] = jnp.sum(rest, axis=0, keepdims=True) + const_ref[0:1]


def grads_kernel(
    g_ref, w0_ref, w1_ref, w2_ref, w3_ref, a_ref, b_ref, c_ref, d_ref, so_far_ref,
    near_ref, far_ref, back_ref, held,
):
    own, x = lax.axis_index("yhi") * 2 + lax.axis_index("core"), lax.axis_index("x")
    hold(held, (a_ref, b_ref, c_ref, d_ref), own)
    zs, feats, rows = g_ref.shape
    grads = g_ref[...].reshape(zs * feats, rows)
    terms = None
    for by, ref in zip(SHIFTS, (w0_ref, w1_ref, w2_ref, w3_ref)):
        q = (x + 4 - by) % 4
        part = contract(grads, ref[...].reshape(zs * feats, LANES), 0, 0)
        term = part * held[q].astype(F32)
        terms = term if terms is None else terms + term
        place = own ^ q

        @pl.when(place == 0)
        def _():
            near_ref[...] = part

        @pl.when(place == 2)
        def _():
            far_ref[0:rows] = part

        @pl.when(place % 2 == 1)
        def _():
            back_ref[place // 2, 0:rows] = part

    bound = row_sums(terms) + so_far_ref[...]
    for ref in (far_ref, back_ref.at[1]):
        ref[rows : rows + 8] = jnp.zeros((8, LANES), F32)
        ref[rows : rows + 8, 0:rows] = bound
    back_ref[0, rows : rows + 8] = jnp.zeros((8, LANES), F32)


def their_kernel(far_ref, got_ref, out_ref, bound_ref):
    rows = far_ref.shape[0] - 8
    total = far_ref[...] + got_ref[1]
    bound_ref[...] = total[rows : rows + 8]
    tail = jnp.concatenate([*pieces(total[rows : rows + 1]), jnp.zeros((5, LANES), F32)], axis=0)
    out_ref[...] = jnp.concatenate([total[0:rows], tail], axis=0).astype(BF16)


def backward_kernel(
    label_ref, offset_ref, a_ref, b_ref, c_ref, d_ref, weight_ref, extra_ref,
    status_ref, bounds_ref, slopes_ref, bias_ref, coeffs_ref, near_ref, got_ref, their_ref, bound_ref,
    mine_ref, other_ref, back,
):
    step = pl.program_id(0)
    yhi, z, core = (lax.axis_index(n) for n in NEU)
    domains = status_ref.shape[0]
    select = selector(label_ref[...], offset_ref[...])

    @pl.when(step == 0)
    def _():
        coeffs = coeffs_ref[...]
        rows = coeffs.shape[0]
        their = their_ref[...].astype(F32)
        grads = near_ref[...] + got_ref[0, 0:rows] + their[0:rows] + bias_ref[...]
        factor, offset, chosen = relax_rows(
            coeffs, status_ref[...], bounds_ref[:, 0].astype(F32), bounds_ref[:, 1].astype(F32), slopes_ref[...]
        )
        back[...] = (grads * factor + offset).astype(BF16)
        mine_ref[16:24] = jnp.zeros((8, LANES), F32)
        mine_ref[16:17] = jnp.sum(grads * coeffs * chosen, axis=0, keepdims=True)
        mine_ref[17:18] = bound_ref[0:1] + their[rows : rows + 1] + their[rows + 1 : rows + 2] + their[rows + 2 : rows + 3]

    zs = a_ref.shape[0]
    for k in range(zs):
        for place, ref in enumerate((a_ref, b_ref, c_ref, d_ref)):
            y = yhi if place % 2 == 0 else 1 - yhi
            c = core if place // 2 == 0 else 1 - core
            block = ref[k]
            _, _, _, _, unsplit = decode(block, domains)
            coeffs = contract(select, block, 0, 0)
            kept = jnp.maximum(coeffs, 0.0) * spread(jnp.where(unsplit, 1.0, 0.0))
            grads = contract(back[...], weight_ref[y, k, c], 1, 1)
            summed = jnp.sum(grads * kept, axis=0, keepdims=True)
            if place == 0:
                summed = summed + jnp.where(step * zs + k == z, 1.0, 0.0) * extra_ref[...]
            out = mine_ref if place // 2 == 0 else other_ref
            out[pl.ds(y * 8 + step * zs + k, 1)] = summed


def send_z_kernel(mine_ref, got_ref, out_ref):
    deep = mine_ref[0:16] + got_ref[...]
    rest = mine_ref[16:24]
    for k in range(out_ref.shape[0]):
        out_ref[k, 0:16] = deep
        out_ref[k, 16:24] = rest


def send_dom_kernel(got_ref, out_ref, bound_ref):
    total = got_ref[0]
    for k in range(1, got_ref.shape[0]):
        total = total + got_ref[k]
    bound_ref[...] = total[17:18, 0 : bound_ref.shape[1]]
    first = jnp.concatenate([got_ref[k, 16:17] for k in range(got_ref.shape[0])], axis=0)
    for k in range(out_ref.shape[0]):
        out_ref[k, 0:16] = total[0:16]
        out_ref[k, 16:24] = first


def send_core_kernel(got_ref, out_ref, deep_ref, first_ref):
    yhi = lax.axis_index("yhi")
    halves = []
    for y in range(2):
        total = got_ref[y]
        for k in range(1, got_ref.shape[0] // 2):
            total = total + got_ref[2 * k + y]
        halves.append(total)
    deep = halves[0][0:16] + halves[1][0:16]
    deep_ref[...] = deep
    firsts = [half[16:24] for half in halves]
    first_ref[...] = jnp.where(yhi == 0, firsts[0], firsts[1])
    power = jnp.sum(firsts[0] * firsts[0] + firsts[1] * firsts[1], keepdims=True)
    out_ref[0:4] = jnp.broadcast_to(power, (4, LANES))
    out_ref[4:8] = jnp.broadcast_to(jnp.sum(deep * deep, keepdims=True), (4, LANES))


def finish_kernel(mine_ref, got_ref, deep_ref, first_ref, deep_slopes_ref, first_slopes_ref, first_out, deep_out):
    yhi, z = lax.axis_index("yhi"), lax.axis_index("z")
    total = mine_ref[...] + got_ref[...]

    def advance(slopes, gradient, squares):
        root_mean = jnp.sqrt(squares / HIDDEN_SIZE + epsilon)
        return jnp.clip(slopes + step_rate * gradient / root_mean, 0.0, 1.0)

    first_out[...] = advance(first_slopes_ref[...], first_ref[pl.ds(z, 1)], total[0:1])
    deep_out[...] = advance(deep_slopes_ref[...], deep_ref[pl.ds(yhi * 8 + z, 1)], total[4:5])


def whole(shape):
    return pl.BlockSpec(shape, lambda s: (0,) * len(shape))


def shape(dims, kind=F32):
    return jax.ShapeDtypeStruct(dims, kind)


def shifted(value, axis, size, by):
    return lax.ppermute(value, axis, [(i, (i + by) % size) for i in range(size)])


def on_device(
    spec_label, spec_offset, class_rows, deep_weight, deep_bias, deep_status, deep_bounds,
    deep_slopes, first_weight, first_bias, first_status, first_bounds, first_slopes,
    box_center, box_radius,
):
    rows = spec_label.shape[0]
    domains = deep_status.shape[0]
    feats = box_center.shape[0]
    call = functools.partial(
        pl.pallas_call, compiler_params=pltpu.CompilerParams(vmem_limit_bytes=LIMIT)
    )
    vmem, hbm = pl.BlockSpec(), pl.BlockSpec(memory_space=pltpu.HBM)

    message = pl.pallas_call(
        prep_kernel,
        compiler_params=pltpu.CompilerParams(vmem_limit_bytes=58 * 1024 * 1024),
        in_specs=[hbm, hbm, vmem, vmem, hbm],
        out_shape=shape((8, feats + ROWS_ALL, LANES), BF16),
        scratch_shapes=[
            pltpu.VMEM((domains, LANES), jnp.int32),
            pltpu.VMEM((domains, 2, LANES), jnp.int32),
            pltpu.SemaphoreType.DMA((10,)),
        ],
        name="prep",
    )(deep_status, deep_bounds.transpose(1, 0, 2), class_rows, deep_slopes[None], first_weight.T)
    message = lax.all_to_all(message, "z", 0, 0, tiled=True)
    info_a = message[:, feats:]
    info_b = shifted(info_a, "yhi", 2, 1)
    info_c = shifted(info_a, "core", 2, 1)
    info_c, w_own = lax.optimization_barrier((info_c, message[:, :feats]))
    w_all = [w_own, shifted(w_own, "x", 4, 1), shifted(w_own, "x", 4, 3)]

    label, offset = spec_label[None], spec_offset[None]
    weight = deep_weight.reshape(2, 8, 2, LANES, LANES)
    depth = 2
    info_spec = pl.BlockSpec((depth, ROWS_ALL, LANES), lambda s: (s, 0, 0))
    label_specs = [whole((1, rows))] * 2
    layer_specs = [whole((domains, LANES)), whole((domains, 2, LANES)), whole((1, LANES)), whole((1, LANES))]
    layer = (first_status, first_bounds.transpose(1, 0, 2), first_slopes[None], first_bias[None])
    half_spec = lambda other: pl.BlockSpec(
        (1, depth, 2, LANES, LANES), lambda s: (lax.axis_index("yhi") ^ other, s, 0, 0, 0)
    )
    square = whole((rows, LANES))

    total = call(
        near_kernel,
        grid=(8 // depth,),
        in_specs=label_specs + [info_spec] * 2 + [half_spec(0)],
        out_specs=square,
        out_shape=shape((rows, LANES)),
        name="forward_near",
    )(label, offset, info_a, info_c, weight)
    own_const, extra = call(
        own_kernel, out_shape=[shape((8, rows)), shape((1, LANES))], name="own"
    )(label, offset, info_a, deep_bias[None])
    total, own_const, info_b = lax.optimization_barrier((total, own_const, info_b))
    info_d = shifted(info_b, "core", 2, 1)
    info_d, w_all[2] = lax.optimization_barrier((info_d, w_all[2]))
    w_all.append(shifted(w_all[2], "x", 4, 3))
    sent, coeffs, const = call(
        far_kernel,
        grid=(8 // depth,),
        in_specs=label_specs + [info_spec] * 2 + [half_spec(1), square, whole((8, rows))] + layer_specs,
        out_specs=[square, square, whole((8, rows))],
        out_shape=[shape((rows, LANES), BF16), shape((rows, LANES)), shape((8, rows))],
        scratch_shapes=[pltpu.VMEM((rows, LANES), F32)],
        name="forward_far",
    )(label, offset, info_b, info_d, weight, total, own_const, *layer)

    sent_b = shifted(sent, "yhi", 2, 1)
    sent_c = shifted(sent, "core", 2, 1)
    sent_d = shifted(sent_b, "core", 2, 1)
    sents = (sent, sent_b, sent_c, sent_d)
    held = [pltpu.VMEM((4, rows, LANES), BF16)]
    parts = call(
        input_kernel, out_shape=shape((8, feats, rows), BF16), scratch_shapes=held, name="inputs"
    )(*sents, *w_all)
    parts = lax.all_to_all(parts, "z", 0, 0, tiled=True)
    grads, bound = call(
        box_kernel, out_shape=[shape((8, feats, rows), BF16), shape((1, rows))], name="box"
    )(parts, box_center[None], box_radius[None], const)
    grads = lax.all_to_all(grads, "z", 0, 0, tiled=True)
    near, far, back = call(
        grads_kernel,
        out_shape=[shape((rows, LANES)), shape((rows + 8, LANES)), shape((2, rows + 8, LANES))],
        scratch_shapes=held,
        name="grads",
    )(grads, *w_all, *sents, bound)
    got = shifted(back, "core", 2, 1)
    their, bound = call(
        their_kernel, out_shape=[shape((rows + 8, LANES), BF16), shape((8, LANES))], name="their"
    )(far, got)
    their = shifted(their, "yhi", 2, 1)

    mine, other = call(
        backward_kernel,
        grid=(8 // depth,),
        in_specs=label_specs
        + [info_spec] * 4
        + [pl.BlockSpec((2, depth, 2, LANES, LANES), lambda s: (0, s, 0, 0, 0)), whole((1, LANES))]
        + layer_specs
        + [square, square, pl.BlockSpec((1, rows + 8, LANES), lambda s: (0, 0, 0)), whole((rows + 8, LANES)), whole((8, LANES))],
        out_specs=[whole((24, LANES)), whole((16, LANES))],
        out_shape=[shape((24, LANES)), shape((16, LANES))],
        scratch_shapes=[pltpu.VMEM((rows, LANES), BF16)],
        name="backward",
    )(label, offset, info_a, info_b, info_c, info_d, weight, extra, *layer, coeffs, near, got, their, bound)

    to_z = call(send_z_kernel, out_shape=shape((8, 24, LANES)), name="send_z")(mine, shifted(other, "core", 2, 1))
    got = lax.all_to_all(to_z, "z", 0, 0, tiled=True)
    to_dom, bound = call(
        send_dom_kernel, out_shape=[shape((16, 24, LANES)), shape((1, rows))], name="send_dom"
    )(got)
    got = lax.all_to_all(to_dom, DOM + ("yhi",), 0, 0, tiled=True)
    to_core, deep, first = call(
        send_core_kernel,
        out_shape=[shape((8, LANES)), shape((16, LANES)), shape((8, LANES))],
        name="send_core",
    )(got)
    first_next, deep_next = call(
        finish_kernel, out_shape=[shape((1, LANES)), shape((1, LANES))], name="finish"
    )(to_core, shifted(to_core, "core", 2, 1), deep, first, deep_slopes[None], first_slopes[None])
    return bound[0], first_next[0], deep_next[0]


def solution(mesh):
    fine = Mesh(mesh.devices.reshape(2, 4, 2, 8, 2), DOM + NEU)
    in_specs = (
        P(DOM), P(DOM), P(None, NEU), P(None, NEU), P(NEU), P(DOM, NEU), P(None, DOM, NEU), P(NEU),
        P(None, NEU), P(NEU), P(DOM, NEU), P(None, DOM, NEU), P(NEU), P(NEU), P(NEU),
    )
    out_specs = (P(DOM), P(NEU), P(NEU))
    return jax.shard_map(on_device, mesh=fine, in_specs=in_specs, out_specs=out_specs, check_vma=False)
```

```python
import functools

import jax
import jax.numpy as jnp
from jax import lax
from jax.experimental import pallas as pl
from jax.experimental.pallas import tpu as pltpu
from jax.sharding import Mesh
from jax.sharding import PartitionSpec as P

HIDDEN_SIZE = 8192
CLASSES = 10
GROUP = 8
LANES = 256
LIMIT = 16 * 1024 * 1024

grid_step = 0.0625
step_rate = 0.25
epsilon = 1e-06

ROWS_ALL = 72
CLASS_ROWS = ((0, 30, 2), (2, 59, 5), (7, 64, 3))

DOM = ("ylo", "x")
NEU = ("yhi", "z", "core")
F32, BF16 = jnp.float32, jnp.bfloat16


def spread(per_domain):
    count, width = per_domain.shape
    return jnp.broadcast_to(per_domain[:, None, :], (count, GROUP, width)).reshape(
        count * GROUP, width
    )


def contract(left, right, left_dim, right_dim):
    return lax.dot_general(
        left, right, (((left_dim,), (right_dim,)), ((), ())), preferred_element_type=F32
    )


def selector(label, offset):
    second = label + offset
    second = jnp.where(second >= CLASSES, second - CLASSES, second)
    rows = lax.broadcasted_iota(jnp.int32, (ROWS_ALL, label.shape[1]), 0)
    classes = jnp.full_like(rows, -1)
    for first, at, count in CLASS_ROWS:
        classes = jnp.where((rows >= at) & (rows < at + count), rows - at + first, classes)
    picked = jnp.where(classes == label, 1.0, 0.0) - jnp.where(classes == second, 1.0, 0.0)
    return picked.astype(BF16)


def pieces(values):
    high = lax.reduce_precision(values, 8, 7)
    middle = lax.reduce_precision(values - high, 8, 7)
    return high, middle, (values - high) - middle


def clamped(status, low, up):
    active, unsplit = status == 1, status == 2
    up = jnp.where(unsplit, up, jnp.where(active, 1, 0)).astype(F32)
    low = jnp.where(unsplit, low, jnp.where(active, 0, 1)).astype(F32)
    return low, up


def compose(low, up, classes, slopes):
    return jnp.concatenate(
        [up, *pieces(slopes), classes[0:2], low, classes[2:10], jnp.zeros((5, LANES), F32)], axis=0
    ).astype(BF16)


def decode(block, domains):
    wide = block.astype(F32)
    up, low = wide[0:32][:domains], wide[32:64][:domains]
    slope = wide[27:28] + wide[28:29] + wide[29:30]
    ratio = up / (up + low)
    unsplit = (up > 0.0) & (low > 0.0)
    return up, low, ratio, slope, unsplit


def relax_rows(coeffs, status, low, up, slopes):
    ratio = up / (up + low)
    cept = ratio * (low * grid_step)
    unsplit = status == 2
    fixed = jnp.where(status == 1, 1.0, 0.0)
    at_pos = spread(jnp.where(unsplit, jnp.broadcast_to(slopes, ratio.shape), fixed))
    at_neg = spread(jnp.where(unsplit, ratio, fixed))
    off_neg = spread(jnp.where(unsplit, cept, 0.0))
    on_pos = spread(jnp.where(unsplit, 1.0, 0.0))
    positive = coeffs >= 0.0
    factor = jnp.where(positive, at_pos, at_neg)
    offset = jnp.where(positive, 0.0, off_neg)
    chosen = jnp.where(positive, on_pos, 0.0)
    return factor, offset, chosen


def prep_kernel(status_ref, bounds_ref, class_ref, slopes_ref, weight_ref, out_ref, status, bounds, sems):
    x = lax.axis_index("x")
    count, feats = out_ref.shape[0], weight_ref.shape[0]
    firsts = [
        pltpu.make_async_copy(status_ref, status, sems.at[count]),
        pltpu.make_async_copy(bounds_ref, bounds, sems.at[count + 1]),
    ]
    copies = [
        pltpu.make_async_copy(
            weight_ref.at[:, pl.ds(pl.multiple_of(((x // 2 * count + k) * 2 + x % 2) * LANES, LANES), LANES)],
            out_ref.at[k, pl.ds(0, feats)],
            sems.at[k],
        )
        for k in range(count)
    ]
    for copy in firsts + copies:
        copy.start()
    for copy in firsts:
        copy.wait()
    low, up = clamped(status[...], bounds[:, 0], bounds[:, 1])
    info = compose(low, up, class_ref[...].astype(F32), slopes_ref[...])
    for k in range(count):
        out_ref[k, feats : feats + ROWS_ALL] = info
    for copy in copies:
        copy.wait()


def forward_half(label_ref, offset_ref, own_ref, other_ref, weight_ref, total):
    core = lax.axis_index("core")
    domains = label_ref.shape[1] // GROUP
    select = selector(label_ref[...], offset_ref[...])
    acc = total[...]
    for k in range(own_ref.shape[0]):
        for ref, side in ((own_ref, core), (other_ref, 1 - core)):
            block = ref[k]
            _, _, ratio, slope, unsplit = decode(block, domains)
            coeffs = contract(select, block, 0, 0)
            at_pos = jnp.where(unsplit, jnp.broadcast_to(slope, ratio.shape), ratio)
            factor = jnp.where(coeffs >= 0.0, spread(at_pos), spread(ratio))
            sent = (coeffs * factor).astype(BF16)
            acc = acc + jnp.dot(sent, weight_ref[0, k, side], preferred_element_type=F32)
    total[...] = acc


def own_kernel(label_ref, offset_ref, info_ref, bias_ref, const_ref, extra_ref):
    domains = label_ref.shape[1] // GROUP
    block = info_ref[lax.axis_index("z")]
    _, low, ratio, slope, unsplit = decode(block, domains)
    coeffs = contract(selector(label_ref[...], offset_ref[...]), block, 0, 0)
    at_pos = jnp.where(unsplit, jnp.broadcast_to(slope, ratio.shape), ratio)
    positive = coeffs >= 0.0
    sent = (coeffs * jnp.where(positive, spread(at_pos), spread(ratio))).astype(BF16)
    cept = spread(jnp.where(unsplit, ratio * (low * grid_step), 0.0))
    const_ref[...] = row_sums(sent.astype(F32) * bias_ref[...] + jnp.where(positive, 0.0, coeffs * cept))
    kept = jnp.maximum(coeffs, 0.0) * spread(jnp.where(unsplit, 1.0, 0.0))
    extra_ref[...] = jnp.sum(kept, axis=0, keepdims=True) * bias_ref[...]


def near_kernel(label_ref, offset_ref, own_ref, other_ref, weight_ref, total_ref):
    @pl.when(pl.program_id(0) == 0)
    def _():
        total_ref[...] = jnp.zeros_like(total_ref)

    forward_half(label_ref, offset_ref, own_ref, other_ref, weight_ref, total_ref)


def far_kernel(
    label_ref, offset_ref, own_ref, other_ref, weight_ref, so_far_ref, own_const_ref,
    status_ref, bounds_ref, slopes_ref, bias_ref, sent_ref, coeffs_ref, const_ref, total,
):
    @pl.when(pl.program_id(0) == 0)
    def _():
        total[...] = so_far_ref[...]

    forward_half(label_ref, offset_ref, own_ref, other_ref, weight_ref, total)

    @pl.when(pl.program_id(0) == pl.num_programs(0) - 1)
    def _():
        coeffs = total[...]
        factor, offset, _ = relax_rows(
            coeffs, status_ref[...], bounds_ref[:, 0].astype(F32), bounds_ref[:, 1].astype(F32), slopes_ref[...]
        )
        sent = (coeffs * factor).astype(BF16)
        sent_ref[...] = sent
        coeffs_ref[...] = coeffs
        const_ref[...] = own_const_ref[...] + row_sums(sent.astype(F32) * bias_ref[...] + coeffs * offset)


def row_sums(values):
    return lax.dot_general(
        jnp.ones((8, values.shape[1]), F32), values, (((1,), (1,)), ((), ())),
        precision=lax.Precision.HIGHEST, preferred_element_type=F32,
    )


def hold(held, refs, own):
    for place, ref in enumerate(refs):
        held[own ^ ((place % 2) * 2 + place // 2)] = ref[...]


SHIFTS = (0, 1, 3, 2)


def weights(w0_ref, w1_ref, w2_ref, low_ref, high_ref):
    last = jnp.concatenate([low_ref[...], high_ref[...]], axis=0)
    return [block.reshape(-1, LANES) for block in (w0_ref[...], w1_ref[...], w2_ref[...], last)]


def input_kernel(a_ref, b_ref, c_ref, d_ref, w0_ref, w1_ref, w2_ref, w3_ref, w4_ref, out_ref, held):
    own, x = lax.axis_index("yhi") * 2 + lax.axis_index("core"), lax.axis_index("x")
    hold(held, (a_ref, b_ref, c_ref, d_ref), own)
    zs, feats, _ = w0_ref.shape
    acc = None
    for by, weight in zip(SHIFTS, weights(w0_ref, w1_ref, w2_ref, w3_ref, w4_ref)):
        part = contract(weight, held[(x + 4 - by) % 4], 1, 1)
        acc = part if acc is None else acc + part
    out_ref[...] = acc.reshape(zs, feats, acc.shape[1]).astype(BF16)


def column(row):
    count = row.shape[1]
    down = lax.broadcasted_iota(jnp.int32, (count, count), 0)
    across = lax.broadcasted_iota(jnp.int32, (count, count), 1)
    return jnp.sum(jnp.where(down == across, row, 0.0), axis=1, keepdims=True)


def box_kernel(parts_ref, center_ref, radius_ref, const_ref, grads_ref, bound_ref):
    coeffs = parts_ref[0].astype(F32)
    for k in range(1, parts_ref.shape[0]):
        coeffs = coeffs + parts_ref[k].astype(F32)
    center, radius = column(center_ref[...]), column(radius_ref[...])
    wide = center - jnp.where(coeffs > 0.0, radius, jnp.where(coeffs < 0.0, -radius, 0.0))
    grads = wide.astype(BF16)
    for k in range(grads_ref.shape[0]):
        grads_ref[k] = grads
    rest = coeffs * (wide - grads.astype(F32))
    bound_ref[...] = jnp.sum(rest, axis=0, keepdims=True) + const_ref[0:1]


def grads_kernel(
    g_ref, w0_ref, w1_ref, w2_ref, w3_ref, w4_ref, a_ref, b_ref, c_ref, d_ref, so_far_ref,
    near_ref, far_ref, back_ref, held,
):
    own, x = lax.axis_index("yhi") * 2 + lax.axis_index("core"), lax.axis_index("x")
    hold(held, (a_ref, b_ref, c_ref, d_ref), own)
    zs, feats, rows = g_ref.shape
    grads = g_ref[...].reshape(zs * feats, rows)
    terms = None
    for by, weight in zip(SHIFTS, weights(w0_ref, w1_ref, w2_ref, w3_ref, w4_ref)):
        q = (x + 4 - by) % 4
        part = contract(grads, weight, 0, 0)
        term = part * held[q].astype(F32)
        terms = term if terms is None else terms + term
        place = own ^ q

        @pl.when(place == 0)
        def _():
            near_ref[...] = part

        @pl.when(place == 2)
        def _():
            far_ref[0:rows] = part

        @pl.when(place % 2 == 1)
        def _():
            back_ref[place // 2, 0:rows] = part

    bound = row_sums(terms) + so_far_ref[...]
    for ref in (far_ref, back_ref.at[1]):
        ref[rows : rows + 8] = jnp.zeros((8, LANES), F32)
        ref[rows : rows + 8, 0:rows] = bound
    back_ref[0, rows : rows + 8] = jnp.zeros((8, LANES), F32)


def their_kernel(far_ref, got_ref, out_ref, bound_ref):
    rows = far_ref.shape[0] - 8
    total = far_ref[...] + got_ref[1]
    bound_ref[...] = total[rows : rows + 8]
    tail = jnp.concatenate([*pieces(total[rows : rows + 1]), jnp.zeros((5, LANES), F32)], axis=0)
    out_ref[...] = jnp.concatenate([total[0:rows], tail], axis=0).astype(BF16)


def backward_kernel(
    label_ref, offset_ref, a_ref, b_ref, c_ref, d_ref, weight_ref, extra_ref,
    status_ref, bounds_ref, slopes_ref, bias_ref, coeffs_ref, near_ref, got_ref, their_ref, bound_ref,
    mine_ref, other_ref, back,
):
    step = pl.program_id(0)
    yhi, z, core = (lax.axis_index(n) for n in NEU)
    domains = status_ref.shape[0]
    select = selector(label_ref[...], offset_ref[...])

    @pl.when(step == 0)
    def _():
        coeffs = coeffs_ref[...]
        rows = coeffs.shape[0]
        their = their_ref[...].astype(F32)
        grads = near_ref[...] + got_ref[0, 0:rows] + their[0:rows] + bias_ref[...]
        factor, offset, chosen = relax_rows(
            coeffs, status_ref[...], bounds_ref[:, 0].astype(F32), bounds_ref[:, 1].astype(F32), slopes_ref[...]
        )
        back[...] = (grads * factor + offset).astype(BF16)
        mine_ref[16:24] = jnp.zeros((8, LANES), F32)
        mine_ref[16:17] = jnp.sum(grads * coeffs * chosen, axis=0, keepdims=True)
        mine_ref[17:18] = bound_ref[0:1] + their[rows : rows + 1] + their[rows + 1 : rows + 2] + their[rows + 2 : rows + 3]

    zs = a_ref.shape[0]
    for k in range(zs):
        for place, ref in enumerate((a_ref, b_ref, c_ref, d_ref)):
            y = yhi if place % 2 == 0 else 1 - yhi
            c = core if place // 2 == 0 else 1 - core
            block = ref[k]
            _, _, _, _, unsplit = decode(block, domains)
            coeffs = contract(select, block, 0, 0)
            kept = jnp.maximum(coeffs, 0.0) * spread(jnp.where(unsplit, 1.0, 0.0))
            grads = contract(back[...], weight_ref[y, k, c], 1, 1)
            summed = jnp.sum(grads * kept, axis=0, keepdims=True)
            if place == 0:
                summed = summed + jnp.where(step * zs + k == z, 1.0, 0.0) * extra_ref[...]
            out = mine_ref if place // 2 == 0 else other_ref
            out[pl.ds(y * 8 + step * zs + k, 1)] = summed


def send_z_kernel(mine_ref, got_ref, out_ref):
    deep = mine_ref[0:16] + got_ref[...]
    rest = mine_ref[16:24]
    for k in range(out_ref.shape[0]):
        out_ref[k, 0:16] = deep
        out_ref[k, 16:24] = rest


def send_dom_kernel(got_ref, out_ref, bound_ref):
    total = got_ref[0]
    for k in range(1, got_ref.shape[0]):
        total = total + got_ref[k]
    bound_ref[...] = total[17:18, 0 : bound_ref.shape[1]]
    first = jnp.concatenate([got_ref[k, 16:17] for k in range(got_ref.shape[0])], axis=0)
    for k in range(out_ref.shape[0]):
        out_ref[k, 0:16] = total[0:16]
        out_ref[k, 16:24] = first


def send_core_kernel(got_ref, out_ref, deep_ref, first_ref):
    yhi = lax.axis_index("yhi")
    halves = []
    for y in range(2):
        total = got_ref[y]
        for k in range(1, got_ref.shape[0] // 2):
            total = total + got_ref[2 * k + y]
        halves.append(total)
    deep = halves[0][0:16] + halves[1][0:16]
    deep_ref[...] = deep
    firsts = [half[16:24] for half in halves]
    first_ref[...] = jnp.where(yhi == 0, firsts[0], firsts[1])
    power = jnp.sum(firsts[0] * firsts[0] + firsts[1] * firsts[1], keepdims=True)
    out_ref[0:4] = jnp.broadcast_to(power, (4, LANES))
    out_ref[4:8] = jnp.broadcast_to(jnp.sum(deep * deep, keepdims=True), (4, LANES))


def finish_kernel(mine_ref, got_ref, deep_ref, first_ref, deep_slopes_ref, first_slopes_ref, first_out, deep_out):
    yhi, z = lax.axis_index("yhi"), lax.axis_index("z")
    total = mine_ref[...] + got_ref[...]

    def advance(slopes, gradient, squares):
        root_mean = jnp.sqrt(squares / HIDDEN_SIZE + epsilon)
        return jnp.clip(slopes + step_rate * gradient / root_mean, 0.0, 1.0)

    first_out[...] = advance(first_slopes_ref[...], first_ref[pl.ds(z, 1)], total[0:1])
    deep_out[...] = advance(deep_slopes_ref[...], deep_ref[pl.ds(yhi * 8 + z, 1)], total[4:5])


def whole(shape):
    return pl.BlockSpec(shape, lambda s: (0,) * len(shape))


def shape(dims, kind=F32):
    return jax.ShapeDtypeStruct(dims, kind)


def shifted(value, axis, size, by):
    return lax.ppermute(value, axis, [(i, (i + by) % size) for i in range(size)])


def on_device(
    spec_label, spec_offset, class_rows, deep_weight, deep_bias, deep_status, deep_bounds,
    deep_slopes, first_weight, first_bias, first_status, first_bounds, first_slopes,
    box_center, box_radius,
):
    rows = spec_label.shape[0]
    domains = deep_status.shape[0]
    feats = box_center.shape[0]
    call = functools.partial(
        pl.pallas_call, compiler_params=pltpu.CompilerParams(vmem_limit_bytes=LIMIT)
    )
    vmem, hbm = pl.BlockSpec(), pl.BlockSpec(memory_space=pltpu.HBM)

    message = pl.pallas_call(
        prep_kernel,
        compiler_params=pltpu.CompilerParams(vmem_limit_bytes=58 * 1024 * 1024),
        in_specs=[hbm, hbm, vmem, vmem, hbm],
        out_shape=shape((8, feats + ROWS_ALL, LANES), BF16),
        scratch_shapes=[
            pltpu.VMEM((domains, LANES), jnp.int32),
            pltpu.VMEM((domains, 2, LANES), jnp.int32),
            pltpu.SemaphoreType.DMA((10,)),
        ],
        name="prep",
    )(deep_status, deep_bounds.transpose(1, 0, 2), class_rows, deep_slopes[None], first_weight.T)
    message = lax.all_to_all(message, "z", 0, 0, tiled=True)
    info_a = message[:, feats:]
    info_b = shifted(info_a, "yhi", 2, 1)
    info_c = shifted(info_a, "core", 2, 1)
    info_c, w_own = lax.optimization_barrier((info_c, message[:, :feats]))
    w_all = [w_own, shifted(w_own, "x", 4, 1), shifted(w_own, "x", 4, 3)]

    label, offset = spec_label[None], spec_offset[None]
    weight = deep_weight.reshape(2, 8, 2, LANES, LANES)
    depth = 2
    info_spec = pl.BlockSpec((depth, ROWS_ALL, LANES), lambda s: (s, 0, 0))
    label_specs = [whole((1, rows))] * 2
    layer_specs = [whole((domains, LANES)), whole((domains, 2, LANES)), whole((1, LANES)), whole((1, LANES))]
    layer = (first_status, first_bounds.transpose(1, 0, 2), first_slopes[None], first_bias[None])
    half_spec = lambda other: pl.BlockSpec(
        (1, depth, 2, LANES, LANES), lambda s: (lax.axis_index("yhi") ^ other, s, 0, 0, 0)
    )
    square = whole((rows, LANES))

    total = call(
        near_kernel,
        grid=(8 // depth,),
        in_specs=label_specs + [info_spec] * 2 + [half_spec(0)],
        out_specs=square,
        out_shape=shape((rows, LANES)),
        name="forward_near",
    )(label, offset, info_a, info_c, weight)
    own_const, extra = call(
        own_kernel, out_shape=[shape((8, rows)), shape((1, LANES))], name="own"
    )(label, offset, info_a, deep_bias[None])
    total, own_const, info_b = lax.optimization_barrier((total, own_const, info_b))
    info_d = shifted(info_b, "core", 2, 1)
    sent, coeffs, const = call(
        far_kernel,
        grid=(8 // depth,),
        in_specs=label_specs + [info_spec] * 2 + [half_spec(1), square, whole((8, rows))] + layer_specs,
        out_specs=[square, square, whole((8, rows))],
        out_shape=[shape((rows, LANES), BF16), shape((rows, LANES)), shape((8, rows))],
        scratch_shapes=[pltpu.VMEM((rows, LANES), F32)],
        name="forward_far",
    )(label, offset, info_b, info_d, weight, total, own_const, *layer)

    sent, w_all[1], w_all[2] = lax.optimization_barrier((sent, w_all[1], w_all[2]))
    w_all += [shifted(w_all[1][:4], "x", 4, 1), shifted(w_all[2][4:], "x", 4, 3)]
    sent_b = shifted(sent, "yhi", 2, 1)
    sent_c = shifted(sent, "core", 2, 1)
    sent_d = shifted(sent_b, "core", 2, 1)
    sents = (sent, sent_b, sent_c, sent_d)
    held = [pltpu.VMEM((4, rows, LANES), BF16)]
    parts = call(
        input_kernel, out_shape=shape((8, feats, rows), BF16), scratch_shapes=held, name="inputs"
    )(*sents, *w_all)
    parts = lax.all_to_all(parts, "z", 0, 0, tiled=True)
    grads, bound = call(
        box_kernel, out_shape=[shape((8, feats, rows), BF16), shape((1, rows))], name="box"
    )(parts, box_center[None], box_radius[None], const)
    grads = lax.all_to_all(grads, "z", 0, 0, tiled=True)
    near, far, back = call(
        grads_kernel,
        out_shape=[shape((rows, LANES)), shape((rows + 8, LANES)), shape((2, rows + 8, LANES))],
        scratch_shapes=held,
        name="grads",
    )(grads, *w_all, *sents, bound)
    got = shifted(back, "core", 2, 1)
    their, bound = call(
        their_kernel, out_shape=[shape((rows + 8, LANES), BF16), shape((8, LANES))], name="their"
    )(far, got)
    their = shifted(their, "yhi", 2, 1)

    mine, other = call(
        backward_kernel,
        grid=(8 // depth,),
        in_specs=label_specs
        + [info_spec] * 4
        + [pl.BlockSpec((2, depth, 2, LANES, LANES), lambda s: (0, s, 0, 0, 0)), whole((1, LANES))]
        + layer_specs
        + [square, square, pl.BlockSpec((1, rows + 8, LANES), lambda s: (0, 0, 0)), whole((rows + 8, LANES)), whole((8, LANES))],
        out_specs=[whole((24, LANES)), whole((16, LANES))],
        out_shape=[shape((24, LANES)), shape((16, LANES))],
        scratch_shapes=[pltpu.VMEM((rows, LANES), BF16)],
        name="backward",
    )(label, offset, info_a, info_b, info_c, info_d, weight, extra, *layer, coeffs, near, got, their, bound)

    to_z = call(send_z_kernel, out_shape=shape((8, 24, LANES)), name="send_z")(mine, shifted(other, "core", 2, 1))
    got = lax.all_to_all(to_z, "z", 0, 0, tiled=True)
    to_dom, bound = call(
        send_dom_kernel, out_shape=[shape((16, 24, LANES)), shape((1, rows))], name="send_dom"
    )(got)
    got = lax.all_to_all(to_dom, DOM + ("yhi",), 0, 0, tiled=True)
    to_core, deep, first = call(
        send_core_kernel,
        out_shape=[shape((8, LANES)), shape((16, LANES)), shape((8, LANES))],
        name="send_core",
    )(got)
    first_next, deep_next = call(
        finish_kernel, out_shape=[shape((1, LANES)), shape((1, LANES))], name="finish"
    )(to_core, shifted(to_core, "core", 2, 1), deep, first, deep_slopes[None], first_slopes[None])
    return bound[0], first_next[0], deep_next[0]


def solution(mesh):
    fine = Mesh(mesh.devices.reshape(2, 4, 2, 8, 2), DOM + NEU)
    in_specs = (
        P(DOM), P(DOM), P(None, NEU), P(None, NEU), P(NEU), P(DOM, NEU), P(None, DOM, NEU), P(NEU),
        P(None, NEU), P(NEU), P(DOM, NEU), P(None, DOM, NEU), P(NEU), P(NEU), P(NEU),
    )
    out_specs = (P(DOM), P(NEU), P(NEU))
    return jax.shard_map(on_device, mesh=fine, in_specs=in_specs, out_specs=out_specs, check_vma=False)
```

```python
import functools

import jax
import jax.numpy as jnp
from jax import lax
from jax.experimental import pallas as pl
from jax.experimental.pallas import tpu as pltpu
from jax.sharding import Mesh
from jax.sharding import PartitionSpec as P

HIDDEN_SIZE = 8192
CLASSES = 10
GROUP = 8
LANES = 256
LIMIT = 16 * 1024 * 1024

grid_step = 0.0625
step_rate = 0.25
epsilon = 1e-06

ROWS_ALL = 72
CLASS_ROWS = ((0, 30, 2), (2, 59, 5), (7, 64, 3))

DOM = ("ylo", "x")
NEU = ("yhi", "z", "core")
F32, BF16 = jnp.float32, jnp.bfloat16


def spread(per_domain):
    count, width = per_domain.shape
    return jnp.broadcast_to(per_domain[:, None, :], (count, GROUP, width)).reshape(
        count * GROUP, width
    )


def contract(left, right, left_dim, right_dim):
    return lax.dot_general(
        left, right, (((left_dim,), (right_dim,)), ((), ())), preferred_element_type=F32
    )


def selector(label, offset):
    second = label + offset
    second = jnp.where(second >= CLASSES, second - CLASSES, second)
    rows = lax.broadcasted_iota(jnp.int32, (ROWS_ALL, label.shape[1]), 0)
    classes = jnp.full_like(rows, -1)
    for first, at, count in CLASS_ROWS:
        classes = jnp.where((rows >= at) & (rows < at + count), rows - at + first, classes)
    picked = jnp.where(classes == label, 1.0, 0.0) - jnp.where(classes == second, 1.0, 0.0)
    return picked.astype(BF16)


def pieces(values):
    high = lax.reduce_precision(values, 8, 7)
    middle = lax.reduce_precision(values - high, 8, 7)
    return high, middle, (values - high) - middle


def clamped(status, low, up):
    active, unsplit = status == 1, status == 2
    up = jnp.where(unsplit, up, jnp.where(active, 1, 0)).astype(F32)
    low = jnp.where(unsplit, low, jnp.where(active, 0, 1)).astype(F32)
    return low, up


def compose(low, up, classes, slopes):
    return jnp.concatenate(
        [up, *pieces(slopes), classes[0:2], low, classes[2:10], jnp.zeros((5, LANES), F32)], axis=0
    ).astype(BF16)


def decode(block, domains):
    wide = block.astype(F32)
    up, low = wide[0:32][:domains], wide[32:64][:domains]
    slope = wide[27:28] + wide[28:29] + wide[29:30]
    ratio = up / (up + low)
    unsplit = (up > 0.0) & (low > 0.0)
    return up, low, ratio, slope, unsplit


def relax_rows(coeffs, status, low, up, slopes):
    ratio = up / (up + low)
    cept = ratio * (low * grid_step)
    unsplit = status == 2
    fixed = jnp.where(status == 1, 1.0, 0.0)
    at_pos = spread(jnp.where(unsplit, jnp.broadcast_to(slopes, ratio.shape), fixed))
    at_neg = spread(jnp.where(unsplit, ratio, fixed))
    off_neg = spread(jnp.where(unsplit, cept, 0.0))
    on_pos = spread(jnp.where(unsplit, 1.0, 0.0))
    positive = coeffs >= 0.0
    factor = jnp.where(positive, at_pos, at_neg)
    offset = jnp.where(positive, 0.0, off_neg)
    chosen = jnp.where(positive, on_pos, 0.0)
    return factor, offset, chosen


def prep_kernel(status_ref, bounds_ref, class_ref, slopes_ref, weight_ref, out_ref, status, bounds, sems):
    x = lax.axis_index("x")
    count, feats = out_ref.shape[0], weight_ref.shape[0]
    firsts = [
        pltpu.make_async_copy(status_ref, status, sems.at[count]),
        pltpu.make_async_copy(bounds_ref, bounds, sems.at[count + 1]),
    ]
    copies = [
        pltpu.make_async_copy(
            weight_ref.at[:, pl.ds(pl.multiple_of(((x // 2 * count + k) * 2 + x % 2) * LANES, LANES), LANES)],
            out_ref.at[k, pl.ds(0, feats)],
            sems.at[k],
        )
        for k in range(count)
    ]
    for copy in firsts + copies:
        copy.start()
    for copy in firsts:
        copy.wait()
    low, up = clamped(status[...], bounds[:, 0], bounds[:, 1])
    info = compose(low, up, class_ref[...].astype(F32), slopes_ref[...])
    for k in range(count):
        out_ref[k, feats : feats + ROWS_ALL] = info
    for copy in copies:
        copy.wait()


def forward_half(label_ref, offset_ref, own_ref, other_ref, weight_ref, flip, total):
    core = lax.axis_index("core")
    domains = label_ref.shape[1] // GROUP
    select = selector(label_ref[...], offset_ref[...])
    half = lax.axis_index("yhi") ^ flip

    def step(pair, carry):
        acc = total[...]
        for k in (2 * pair, 2 * pair + 1):
            for ref, side in ((own_ref, core), (other_ref, 1 - core)):
                block = ref[k]
                _, _, ratio, slope, unsplit = decode(block, domains)
                coeffs = contract(select, block, 0, 0)
                at_pos = jnp.where(unsplit, jnp.broadcast_to(slope, ratio.shape), ratio)
                factor = jnp.where(coeffs >= 0.0, spread(at_pos), spread(ratio))
                sent = (coeffs * factor).astype(BF16)
                acc = acc + jnp.dot(sent, weight_ref[half, k, side], preferred_element_type=F32)
        total[...] = acc
        return carry

    lax.fori_loop(0, own_ref.shape[0] // 2, step, 0, unroll=True)


def own_kernel(label_ref, offset_ref, info_ref, bias_ref, const_ref, extra_ref):
    domains = label_ref.shape[1] // GROUP
    block = info_ref[lax.axis_index("z")]
    _, low, ratio, slope, unsplit = decode(block, domains)
    coeffs = contract(selector(label_ref[...], offset_ref[...]), block, 0, 0)
    at_pos = jnp.where(unsplit, jnp.broadcast_to(slope, ratio.shape), ratio)
    positive = coeffs >= 0.0
    sent = (coeffs * jnp.where(positive, spread(at_pos), spread(ratio))).astype(BF16)
    cept = spread(jnp.where(unsplit, ratio * (low * grid_step), 0.0))
    const_ref[...] = row_sums(sent.astype(F32) * bias_ref[...] + jnp.where(positive, 0.0, coeffs * cept))
    kept = jnp.maximum(coeffs, 0.0) * spread(jnp.where(unsplit, 1.0, 0.0))
    extra_ref[...] = jnp.sum(kept, axis=0, keepdims=True) * bias_ref[...]


def near_kernel(label_ref, offset_ref, own_ref, other_ref, weight_ref, total_ref):
    total_ref[...] = jnp.zeros_like(total_ref)
    forward_half(label_ref, offset_ref, own_ref, other_ref, weight_ref, 0, total_ref)


def far_kernel(
    label_ref, offset_ref, own_ref, other_ref, weight_ref, so_far_ref, own_const_ref,
    status_ref, bounds_ref, slopes_ref, bias_ref, sent_ref, coeffs_ref, const_ref,
):
    coeffs_ref[...] = so_far_ref[...]
    forward_half(label_ref, offset_ref, own_ref, other_ref, weight_ref, 1, coeffs_ref)
    coeffs = coeffs_ref[...]
    factor, offset, _ = relax_rows(
        coeffs, status_ref[...], bounds_ref[:, 0].astype(F32), bounds_ref[:, 1].astype(F32), slopes_ref[...]
    )
    sent = (coeffs * factor).astype(BF16)
    sent_ref[...] = sent
    const_ref[...] = own_const_ref[...] + row_sums(sent.astype(F32) * bias_ref[...] + coeffs * offset)


def row_sums(values):
    return lax.dot_general(
        jnp.ones((8, values.shape[1]), F32), values, (((1,), (1,)), ((), ())),
        precision=lax.Precision.HIGHEST, preferred_element_type=F32,
    )


def hold(held, refs, own):
    for place, ref in enumerate(refs):
        held[own ^ ((place % 2) * 2 + place // 2)] = ref[...]


SHIFTS = (0, 1, 3, 2)


def weights(w0_ref, w1_ref, w2_ref, low_ref, high_ref):
    last = jnp.concatenate([low_ref[...], high_ref[...]], axis=0)
    return [block.reshape(-1, LANES) for block in (w0_ref[...], w1_ref[...], w2_ref[...], last)]


def input_kernel(a_ref, b_ref, c_ref, d_ref, w0_ref, w1_ref, w2_ref, w3_ref, w4_ref, out_ref, held):
    own, x = lax.axis_index("yhi") * 2 + lax.axis_index("core"), lax.axis_index("x")
    hold(held, (a_ref, b_ref, c_ref, d_ref), own)
    zs, feats, _ = w0_ref.shape
    acc = None
    for by, weight in zip(SHIFTS, weights(w0_ref, w1_ref, w2_ref, w3_ref, w4_ref)):
        part = contract(weight, held[(x + 4 - by) % 4], 1, 1)
        acc = part if acc is None else acc + part
    out_ref[...] = acc.reshape(zs, feats, acc.shape[1]).astype(BF16)


def column(row):
    count = row.shape[1]
    down = lax.broadcasted_iota(jnp.int32, (count, count), 0)
    across = lax.broadcasted_iota(jnp.int32, (count, count), 1)
    return jnp.sum(jnp.where(down == across, row, 0.0), axis=1, keepdims=True)


def box_kernel(parts_ref, center_ref, radius_ref, const_ref, grads_ref, bound_ref):
    coeffs = parts_ref[0].astype(F32)
    for k in range(1, parts_ref.shape[0]):
        coeffs = coeffs + parts_ref[k].astype(F32)
    center, radius = column(center_ref[...]), column(radius_ref[...])
    wide = center - jnp.where(coeffs > 0.0, radius, jnp.where(coeffs < 0.0, -radius, 0.0))
    grads = wide.astype(BF16)
    for k in range(grads_ref.shape[0]):
        grads_ref[k] = grads
    rest = coeffs * (wide - grads.astype(F32))
    bound_ref[...] = jnp.sum(rest, axis=0, keepdims=True) + const_ref[0:1]


def grads_kernel(
    g_ref, w0_ref, w1_ref, w2_ref, w3_ref, w4_ref, a_ref, b_ref, c_ref, d_ref, so_far_ref,
    near_ref, far_ref, back_ref, held,
):
    own, x = lax.axis_index("yhi") * 2 + lax.axis_index("core"), lax.axis_index("x")
    hold(held, (a_ref, b_ref, c_ref, d_ref), own)
    zs, feats, rows = g_ref.shape
    grads = g_ref[...].reshape(zs * feats, rows)
    terms = None
    for by, weight in zip(SHIFTS, weights(w0_ref, w1_ref, w2_ref, w3_ref, w4_ref)):
        q = (x + 4 - by) % 4
        part = contract(grads, weight, 0, 0)
        term = part * held[q].astype(F32)
        terms = term if terms is None else terms + term
        place = own ^ q

        @pl.when(place == 0)
        def _():
            near_ref[...] = part

        @pl.when(place == 2)
        def _():
            far_ref[0:rows] = part

        @pl.when(place % 2 == 1)
        def _():
            back_ref[place // 2, 0:rows] = part

    bound = row_sums(terms) + so_far_ref[...]
    for ref in (far_ref, back_ref.at[1]):
        ref[rows : rows + 8] = jnp.zeros((8, LANES), F32)
        ref[rows : rows + 8, 0:rows] = bound
    back_ref[0, rows : rows + 8] = jnp.zeros((8, LANES), F32)


def their_kernel(far_ref, got_ref, out_ref, bound_ref):
    rows = far_ref.shape[0] - 8
    total = far_ref[...] + got_ref[1]
    bound_ref[...] = total[rows : rows + 8]
    tail = jnp.concatenate([*pieces(total[rows : rows + 1]), jnp.zeros((5, LANES), F32)], axis=0)
    out_ref[...] = jnp.concatenate([total[0:rows], tail], axis=0).astype(BF16)


def backward_kernel(
    label_ref, offset_ref, a_ref, b_ref, c_ref, d_ref, weight_ref, extra_ref,
    status_ref, bounds_ref, slopes_ref, bias_ref, coeffs_ref, near_ref, got_ref, their_ref, bound_ref,
    mine_ref, other_ref, back,
):
    yhi, z, core = (lax.axis_index(n) for n in NEU)
    domains = status_ref.shape[0]
    select = selector(label_ref[...], offset_ref[...])

    coeffs = coeffs_ref[...]
    rows = coeffs.shape[0]
    their = their_ref[...].astype(F32)
    grads = near_ref[...] + got_ref[0, 0:rows] + their[0:rows] + bias_ref[...]
    factor, offset, chosen = relax_rows(
        coeffs, status_ref[...], bounds_ref[:, 0].astype(F32), bounds_ref[:, 1].astype(F32), slopes_ref[...]
    )
    back[...] = (grads * factor + offset).astype(BF16)
    mine_ref[16:24] = jnp.zeros((8, LANES), F32)
    mine_ref[16:17] = jnp.sum(grads * coeffs * chosen, axis=0, keepdims=True)
    mine_ref[17:18] = bound_ref[0:1] + their[rows : rows + 1] + their[rows + 1 : rows + 2] + their[rows + 2 : rows + 3]

    def step(pair, carry):
        for k in (2 * pair, 2 * pair + 1):
            for place, ref in enumerate((a_ref, b_ref, c_ref, d_ref)):
                y = yhi if place % 2 == 0 else 1 - yhi
                c = core if place // 2 == 0 else 1 - core
                block = ref[k]
                _, _, _, _, unsplit = decode(block, domains)
                coeffs = contract(select, block, 0, 0)
                kept = jnp.maximum(coeffs, 0.0) * spread(jnp.where(unsplit, 1.0, 0.0))
                grads = contract(back[...], weight_ref[y, k, c], 1, 1)
                summed = jnp.sum(grads * kept, axis=0, keepdims=True)
                if place == 0:
                    summed = summed + jnp.where(k == z, 1.0, 0.0) * extra_ref[...]
                out = mine_ref if place // 2 == 0 else other_ref
                out[pl.ds(y * 8 + k, 1)] = summed
        return carry

    lax.fori_loop(0, a_ref.shape[0] // 2, step, 0, unroll=True)


def send_z_kernel(mine_ref, got_ref, out_ref):
    deep = mine_ref[0:16] + got_ref[...]
    rest = mine_ref[16:24]
    for k in range(out_ref.shape[0]):
        out_ref[k, 0:16] = deep
        out_ref[k, 16:24] = rest


def send_dom_kernel(got_ref, out_ref, bound_ref):
    total = got_ref[0]
    for k in range(1, got_ref.shape[0]):
        total = total + got_ref[k]
    bound_ref[...] = total[17:18, 0 : bound_ref.shape[1]]
    first = jnp.concatenate([got_ref[k, 16:17] for k in range(got_ref.shape[0])], axis=0)
    for k in range(out_ref.shape[0]):
        out_ref[k, 0:16] = total[0:16]
        out_ref[k, 16:24] = first


def send_core_kernel(got_ref, out_ref, deep_ref, first_ref):
    yhi = lax.axis_index("yhi")
    halves = []
    for y in range(2):
        total = got_ref[y]
        for k in range(1, got_ref.shape[0] // 2):
            total = total + got_ref[2 * k + y]
        halves.append(total)
    deep = halves[0][0:16] + halves[1][0:16]
    deep_ref[...] = deep
    firsts = [half[16:24] for half in halves]
    first_ref[...] = jnp.where(yhi == 0, firsts[0], firsts[1])
    power = jnp.sum(firsts[0] * firsts[0] + firsts[1] * firsts[1], keepdims=True)
    out_ref[0:4] = jnp.broadcast_to(power, (4, LANES))
    out_ref[4:8] = jnp.broadcast_to(jnp.sum(deep * deep, keepdims=True), (4, LANES))


def finish_kernel(mine_ref, got_ref, deep_ref, first_ref, deep_slopes_ref, first_slopes_ref, first_out, deep_out):
    yhi, z = lax.axis_index("yhi"), lax.axis_index("z")
    total = mine_ref[...] + got_ref[...]

    def advance(slopes, gradient, squares):
        root_mean = jnp.sqrt(squares / HIDDEN_SIZE + epsilon)
        return jnp.clip(slopes + step_rate * gradient / root_mean, 0.0, 1.0)

    first_out[...] = advance(first_slopes_ref[...], first_ref[pl.ds(z, 1)], total[0:1])
    deep_out[...] = advance(deep_slopes_ref[...], deep_ref[pl.ds(yhi * 8 + z, 1)], total[4:5])


def shape(dims, kind=F32):
    return jax.ShapeDtypeStruct(dims, kind)


def shifted(value, axis, size, by):
    return lax.ppermute(value, axis, [(i, (i + by) % size) for i in range(size)])


def on_device(
    spec_label, spec_offset, class_rows, deep_weight, deep_bias, deep_status, deep_bounds,
    deep_slopes, first_weight, first_bias, first_status, first_bounds, first_slopes,
    box_center, box_radius,
):
    rows = spec_label.shape[0]
    domains = deep_status.shape[0]
    feats = box_center.shape[0]
    call = functools.partial(
        pl.pallas_call, compiler_params=pltpu.CompilerParams(vmem_limit_bytes=LIMIT)
    )
    vmem, hbm = pl.BlockSpec(), pl.BlockSpec(memory_space=pltpu.HBM)

    message = pl.pallas_call(
        prep_kernel,
        compiler_params=pltpu.CompilerParams(vmem_limit_bytes=58 * 1024 * 1024),
        in_specs=[hbm, hbm, vmem, vmem, hbm],
        out_shape=shape((8, feats + ROWS_ALL, LANES), BF16),
        scratch_shapes=[
            pltpu.VMEM((domains, LANES), jnp.int32),
            pltpu.VMEM((domains, 2, LANES), jnp.int32),
            pltpu.SemaphoreType.DMA((10,)),
        ],
        name="prep",
    )(deep_status, deep_bounds.transpose(1, 0, 2), class_rows, deep_slopes[None], first_weight.T)
    message = lax.all_to_all(message, "z", 0, 0, tiled=True)
    info_a = message[:, feats:]
    info_b = shifted(info_a, "yhi", 2, 1)
    info_c = shifted(info_a, "core", 2, 1)
    info_c, w_own = lax.optimization_barrier((info_c, message[:, :feats]))
    w_all = [w_own, shifted(w_own, "x", 4, 1), shifted(w_own, "x", 4, 3)]

    label, offset = spec_label[None], spec_offset[None]
    weight = deep_weight.reshape(2, 8, 2, LANES, LANES)
    layer = (first_status, first_bounds.transpose(1, 0, 2), first_slopes[None], first_bias[None])
    total = call(
        near_kernel,
        out_shape=shape((rows, LANES)),
        name="forward_near",
    )(label, offset, info_a, info_c, weight)
    own_const, extra = call(
        own_kernel, out_shape=[shape((8, rows)), shape((1, LANES))], name="own"
    )(label, offset, info_a, deep_bias[None])
    total, own_const, info_b = lax.optimization_barrier((total, own_const, info_b))
    info_d = shifted(info_b, "core", 2, 1)
    sent, coeffs, const = call(
        far_kernel,
        out_shape=[shape((rows, LANES), BF16), shape((rows, LANES)), shape((8, rows))],
        name="forward_far",
    )(label, offset, info_b, info_d, weight, total, own_const, *layer)

    sent, w_all[1], w_all[2] = lax.optimization_barrier((sent, w_all[1], w_all[2]))
    w_all += [shifted(w_all[1][:4], "x", 4, 1), shifted(w_all[2][4:], "x", 4, 3)]
    sent_b = shifted(sent, "yhi", 2, 1)
    sent_c = shifted(sent, "core", 2, 1)
    sent_d = shifted(sent_b, "core", 2, 1)
    sents = (sent, sent_b, sent_c, sent_d)
    held = [pltpu.VMEM((4, rows, LANES), BF16)]
    parts = call(
        input_kernel, out_shape=shape((8, feats, rows), BF16), scratch_shapes=held, name="inputs"
    )(*sents, *w_all)
    parts = lax.all_to_all(parts, "z", 0, 0, tiled=True)
    grads, bound = call(
        box_kernel, out_shape=[shape((8, feats, rows), BF16), shape((1, rows))], name="box"
    )(parts, box_center[None], box_radius[None], const)
    grads = lax.all_to_all(grads, "z", 0, 0, tiled=True)
    near, far, back = call(
        grads_kernel,
        out_shape=[shape((rows, LANES)), shape((rows + 8, LANES)), shape((2, rows + 8, LANES))],
        scratch_shapes=held,
        name="grads",
    )(grads, *w_all, *sents, bound)
    got = shifted(back, "core", 2, 1)
    their, bound = call(
        their_kernel, out_shape=[shape((rows + 8, LANES), BF16), shape((8, LANES))], name="their"
    )(far, got)
    their = shifted(their, "yhi", 2, 1)

    mine, other = call(
        backward_kernel,
        out_shape=[shape((24, LANES)), shape((16, LANES))],
        scratch_shapes=[pltpu.VMEM((rows, LANES), BF16)],
        name="backward",
    )(label, offset, info_a, info_b, info_c, info_d, weight, extra, *layer, coeffs, near, got, their, bound)

    to_z = call(send_z_kernel, out_shape=shape((8, 24, LANES)), name="send_z")(mine, shifted(other, "core", 2, 1))
    got = lax.all_to_all(to_z, "z", 0, 0, tiled=True)
    to_dom, bound = call(
        send_dom_kernel, out_shape=[shape((16, 24, LANES)), shape((1, rows))], name="send_dom"
    )(got)
    got = lax.all_to_all(to_dom, DOM + ("yhi",), 0, 0, tiled=True)
    to_core, deep, first = call(
        send_core_kernel,
        out_shape=[shape((8, LANES)), shape((16, LANES)), shape((8, LANES))],
        name="send_core",
    )(got)
    first_next, deep_next = call(
        finish_kernel, out_shape=[shape((1, LANES)), shape((1, LANES))], name="finish"
    )(to_core, shifted(to_core, "core", 2, 1), deep, first, deep_slopes[None], first_slopes[None])
    return bound[0], first_next[0], deep_next[0]


def solution(mesh):
    fine = Mesh(mesh.devices.reshape(2, 4, 2, 8, 2), DOM + NEU)
    in_specs = (
        P(DOM), P(DOM), P(None, NEU), P(None, NEU), P(NEU), P(DOM, NEU), P(None, DOM, NEU), P(NEU),
        P(None, NEU), P(NEU), P(DOM, NEU), P(None, DOM, NEU), P(NEU), P(NEU), P(NEU),
    )
    out_specs = (P(DOM), P(NEU), P(NEU))
    return jax.shard_map(on_device, mesh=fine, in_specs=in_specs, out_specs=out_specs, check_vma=False)
```
